128 devices in a mesh: blk: 16 (over x_hi, z, core), near: 8 (over x_lo, y).
Axes of the slice: x: 4 (x_hi: 2, x_lo: 2; x = x_hi * 2 + x_lo), y: 4, z: 4, core: 2. Of those that a mesh axis runs over, the one named last changes fastest.
Arguments:
- rhs_block: bfloat16 [16, 16, 256, 256], P('blk', 'near'), may hold values from -18 to 18
- far_u: bfloat16 [256, 16, 16, 32, 256], P('blk', None, 'near'), may hold values from -0.09375 to 0.09375
- far_w: bfloat16 [256, 16, 16, 32, 256], P('blk', None, 'near'), may hold values from -0.375 to 0.375
- far_ranks: int32 [256, 16, 16], P('blk', None, 'near'), may hold values from 8 to 32
- near_tiles: bfloat16 [16, 16, 8, 256, 256], P('blk', 'near'), may hold values from -6 to 6
- near_cols: int32 [16, 16, 8], P('blk'), may hold values from 0 to 15, as said below
- near_count: int32 [16, 16], P('blk'), may hold values from 1 to 8, as said below
Outputs:
- second_basis: bfloat16 [16, 16, 256, 256], P('blk', 'near')
- second_image: float32 [16, 16, 256, 256], P('blk', 'near')
- coefficients: float32 [2, 256], replicated
The draws below stay inside these ranges and needn't reach their ends.
Inputs may be any that keep to these rules, and one draw needn't show every extreme that they name: `near_cols`: slot 0 of every block row is the row's own block; the slots of one row name distinct blocks of its panel. `near_count`: some block row has all 8 slots live.
All inputs are finite; a program needn't handle non-finite values.
Results may differ from the reference program's by a relative error of at most 0.015.
Values may be sent and summed in bfloat16 or wider, within the bound.
No kernel may reach another device: no remote copies, remote signals or barrier semaphores. Data moves between devices by JAX's collectives and lax.ppermute only.
A program may use at most 128 MiB of HBM per device.

```python
import jax
import jax.numpy as jnp
from jax import lax

BS = 256
R = 32
RHS = 256
P_DEV = 2
KMAX = 8
PB = 16
PANELS = 16
NB = 256
ROWS = 65536
N_NEAR = 8


def draw_near_cols(key, part):
    key = jax.random.fold_in(key, 11)
    scores = jax.random.randint(key, (PANELS, PB, PB - 1), 0, 1 << 20) * (PB - 1) + jnp.arange(PB - 1, dtype=jnp.int32)
    order = jnp.argsort(scores, axis=-1).astype(jnp.int32) + 1
    offsets = jnp.concatenate([jnp.zeros((PANELS, PB, 1), jnp.int32), order[..., :KMAX - 1]], axis=-1)
    return ((jnp.arange(PB, dtype=jnp.int32)[None, :, None] + offsets) % PB).astype(jnp.int32)


def draw_near_count(key, part):
    key = jax.random.fold_in(key, 23)
    first_key, second_key = jax.random.split(key)
    counts = jax.random.randint(first_key, (PANELS * PB,), 1, KMAX + 1)
    spot = jax.random.randint(second_key, (), 0, PANELS * PB)
    counts = jnp.where(jnp.arange(PANELS * PB, dtype=jnp.int32) == spot, KMAX, counts)
    return counts.reshape(PANELS, PB).astype(jnp.int32)


def scaled_field(key, top):
    level = jnp.arange(PANELS, dtype=jnp.float32) / max(PANELS - 1, 1)
    scale = (1.0 + (top - 1.0) * level)[:, None, None, None]
    noise = jnp.clip(jax.random.normal(key, (PANELS, PB, BS, RHS), jnp.float32), -6.0, 6.0)
    return noise * scale


def draw_rhs_block(key, part):
    key = jax.random.fold_in(key, 37)
    values = scaled_field(key, 3.0)
    return values.astype(jnp.bfloat16)


def draw_near_tiles(key, part):
    key = jax.random.fold_in(key, 41)
    noise_key, diag_key = jax.random.split(key)
    shape = (PANELS, PB, KMAX, BS, BS)
    noise = jnp.clip(jax.random.normal(noise_key, shape, jnp.float32), -4.0, 4.0)
    noise = noise * (1.0 / BS ** 0.5)
    diag = jax.random.uniform(diag_key, (PANELS, PB, 1, BS, 1), jnp.float32, 1.5, 3.5)
    ident = (jnp.arange(BS)[:, None] == jnp.arange(BS)[None, :]).astype(jnp.float32)
    own = (jnp.arange(KMAX) == 0).astype(jnp.float32)[None, None, :, None, None]
    return (noise + own * diag * ident[None, None, None]).astype(jnp.bfloat16)


def place_ends(values, stream_key, least, high):
    longest = values.shape.index(max(values.shape))
    spots = []
    for shift in (0, 1):
        where = [jax.random.randint(jax.random.fold_in(stream_key, axis), (), 0, length) for axis, length in enumerate(values.shape)]
        where[longest] = (where[longest] + shift) % values.shape[longest]
        spots.append(tuple(where))
    return values.at[spots[0]].set(least).at[spots[1]].set(high)


def steps_of(rng, extent, shards, least, largest):
    loudness = 1.0
    for position, blocks in shards:
        steps = jax.random.uniform(jax.random.fold_in(jax.random.fold_in(rng, 6), position), (blocks,), jnp.float32, least / len(shards), largest / len(shards))
        loudness = loudness * jnp.repeat(jnp.exp(steps), extent[position] // blocks).reshape((-1,) + (1,) * (len(extent) - 1 - position))
    return loudness


def scatter_about(key, dims, width, limit, shards=(), held_as=jnp.bfloat16):
    array = jax.random.normal(key, dims, jnp.float32) * width
    if len(shards) > 0:
        array = steps_of(key, dims, shards, -0.22, 0.18) * array
    return jnp.clip(array, min=-limit, max=limit).astype(held_as)


def setup_inputs(seed: int = 0) -> dict:
    arg_keys = jax.random.split(jax.random.key(seed), 8)
    return {
        "rhs_block": draw_rhs_block(jax.random.fold_in(arg_keys[7], 71), 0),
        "far_u": scatter_about(arg_keys[1], (NB, PANELS, PB, R, BS), (NB * R // 2) ** -0.5, 0.09375, ((0, 16), (2, 8))),
        "far_w": scatter_about(arg_keys[2], (NB, PANELS, PB, R, BS), BS ** -0.5, 0.375, ((0, 16), (2, 8))),
        "far_ranks": place_ends(jax.random.randint(arg_keys[3], (NB, PANELS, PB), R // 4, R + 1), jax.random.fold_in(arg_keys[3], 1), R // 4, R).astype(jnp.int32),
        "near_tiles": draw_near_tiles(jax.random.fold_in(arg_keys[7], 71), 0),
        "near_cols": draw_near_cols(jax.random.fold_in(arg_keys[7], 71), 0),
        "near_count": draw_near_count(jax.random.fold_in(arg_keys[7], 71), 0),
    }


def apply_matrix(field, far_u, far_w, far_ranks, near_tiles, near_cols, near_count):
    values = field.astype(jnp.float32)

    def one_target(index):
        panel = index // PB
        local = index % PB
        w_row = far_w[index].astype(jnp.float32)
        u_row = far_u[index].astype(jnp.float32)
        cols = near_cols[panel, local]
        live = jnp.arange(KMAX, dtype=jnp.int32) < near_count[panel, local]
        is_near = jnp.any((cols[:, None] == jnp.arange(PB, dtype=jnp.int32)[None, :]) & live[:, None], axis=0)
        near_pair = (jnp.arange(PANELS, dtype=jnp.int32) == panel)[:, None] & is_near[None, :]
        ranked = jnp.arange(R, dtype=jnp.int32)[None, None, :] < far_ranks[index][..., None]
        keep = (ranked & jnp.logical_not(near_pair)[..., None]).astype(jnp.float32)
        coded = jnp.einsum('bqrs,bqsc->bqrc', w_row, values) * keep[..., None]
        coded = lax.optimization_barrier(coded.astype(jnp.bfloat16)).astype(jnp.float32)
        partial_value = jnp.einsum('bqrs,bqrc->qsc', u_row, coded)
        partial_value = partial_value.reshape(N_NEAR, P_DEV, BS, RHS).sum(axis=1)
        partial_value = lax.optimization_barrier(partial_value.astype(jnp.bfloat16)).astype(jnp.float32)
        sources = values[panel][cols] * live.astype(jnp.float32)[:, None, None]
        near = jnp.einsum('kst,ktc->sc', near_tiles[panel, local].astype(jnp.float32), sources)
        return partial_value.sum(axis=0) + near
    result = lax.map(one_target, jnp.arange(PANELS * PB, dtype=jnp.int32))
    return result.reshape(PANELS, PB, BS, RHS)

def reference(rhs_block, far_u, far_w, far_ranks, near_tiles, near_cols, near_count):
    start = rhs_block.astype(jnp.float32)
    mean_start = lax.optimization_barrier(jnp.sum(start * start, axis=(0, 1, 2))) / ROWS
    first = (start * lax.rsqrt(mean_start + 1e-06)).astype(jnp.bfloat16)
    image = apply_matrix(first, far_u, far_w, far_ranks, near_tiles, near_cols, near_count)
    first_f = first.astype(jnp.float32)
    proj = lax.optimization_barrier(jnp.sum(first_f * image, axis=(0, 1, 2))) / ROWS
    rest = image - proj * first_f
    mean_rest = lax.optimization_barrier(jnp.sum(rest * rest, axis=(0, 1, 2))) / ROWS
    second_basis = (rest * lax.rsqrt(mean_rest + 1e-06)).astype(jnp.bfloat16)
    second_image = apply_matrix(second_basis, far_u, far_w, far_ranks, near_tiles, near_cols, near_count)
    coefficients = jnp.stack([proj, jnp.sqrt(mean_rest + 1e-06)])
    return (second_basis, second_image, coefficients)
```

```python
import functools

import jax
import jax.numpy as jnp
from jax import lax
from jax.experimental import pallas as pl
from jax.experimental.pallas import tpu as pltpu
from jax.sharding import PartitionSpec as P

EPS = 1e-06
EXTRA = 16
MIB = 1 << 20


def put_sums(sums, width):
    rows = []
    for value in sums:
        high = value.astype(jnp.bfloat16)
        left = value - high.astype(jnp.float32)
        middle = left.astype(jnp.bfloat16)
        low = (left - middle.astype(jnp.float32)).astype(jnp.bfloat16)
        rows += [high, middle, low]
    rows.append(jnp.zeros((EXTRA - len(rows), width), jnp.bfloat16))
    return jnp.concatenate(rows, axis=0)


def get_sums(rows):
    return (
        rows[0:1] + rows[1:2] + rows[2:3],
        rows[3:4] + rows[4:5] + rows[5:6],
    )


def whole(shape):
    return pl.BlockSpec(shape, lambda *_: (0,) * len(shape))


def start_kernel(x_ref, own_ref, out_ref):
    copies, rows, width = out_ref.shape
    per_dev, size, _ = x_ref.shape
    square = jnp.zeros((1, width), jnp.float32)
    cross = jnp.zeros((1, width), jnp.float32)
    for p in range(per_dev):
        x = x_ref[p]
        x_f = x.astype(jnp.float32)
        image = jnp.dot(own_ref[p, 0], x, preferred_element_type=jnp.float32)
        square += jnp.sum(x_f * x_f, axis=0, keepdims=True)
        cross += jnp.sum(x_f * image, axis=0, keepdims=True)
        for k in range(copies):
            out_ref[k, p * size : (p + 1) * size, :] = x
    extra = put_sums((square, cross), width)
    for k in range(copies):
        out_ref[k, per_dev * size :, :] = extra


def far_kernel(
    place_ref, rank_ref, w_ref, u_ref, p00, p10, p01, p11, out_ref, coded_ref, sums_ref,
    *, zs, per_dev, targets, rank, size,
):
    step = pl.program_id(0)
    half = 2 * zs
    width = out_ref.shape[2]
    blocks = per_dev * size
    xh, core = place_ref[0], place_ref[1]

    @pl.when(step == 0)
    def _():
        sums_ref[...] = jnp.zeros_like(sums_ref)

    def code(side, mine, other):
        z = step - side * zs
        pair = (jnp.where(side == 1, 1 - xh, xh) * zs + z) * 2
        row = lax.broadcasted_iota(jnp.int32, (rank, width), 0)
        for turn, source in ((0, mine), (1, other)):
            which = core if turn == 0 else 1 - core
            panel = pair + which
            sums_ref[...] += source[0, blocks:, :].astype(jnp.float32)
            for p in range(per_dev):
                w = w_ref[:, which, p].reshape(targets * rank, size)
                field = source[0, p * size : (p + 1) * size, :]
                value = jnp.dot(w, field, preferred_element_type=jnp.float32)
                for i in range(targets):
                    live = rank_ref[panel * per_dev + p, i]
                    part = value[i * rank : (i + 1) * rank]
                    part = jnp.where(row < live, part, 0.0).astype(jnp.bfloat16)
                    coded_ref[i, panel, p * rank : (p + 1) * rank, :] = part

    @pl.when(step < zs)
    def _():
        code(0, p00, p01)

    @pl.when((step >= zs) & (step < half))
    def _():
        code(1, p10, p11)

    @pl.when(step >= half)
    def _():
        first = (step - half) * per_dev
        for p in range(per_dev):
            u = u_ref[p].reshape(-1, size)
            value = coded_ref[first + p].reshape(-1, width)
            total = lax.dot_general(
                u, value, (((0,), (0,)), ((), ())), preferred_element_type=jnp.float32
            )
            out_ref[0, p * size : (p + 1) * size, :] = total.astype(jnp.bfloat16)
        out_ref[0, blocks:, :] = put_sums(get_sums(sums_ref[...]), width)


def row_image(cols_ref, count_ref, far_ref, tiles_ref, panel_ref, p, total_ref):
    size = tiles_ref.shape[2]
    senders = far_ref.shape[0]
    total = far_ref[0, p * size : (p + 1) * size, :].astype(jnp.float32)
    for s in range(1, senders):
        total += far_ref[s, p * size : (p + 1) * size, :].astype(jnp.float32)
    total_ref[...] = total
    for k in range(tiles_ref.shape[1]):

        @pl.when(k < count_ref[p])
        def _():
            total_ref[...] += jnp.dot(
                tiles_ref[p, k], panel_ref[cols_ref[p, k]], preferred_element_type=jnp.float32
            )

    return total_ref[...]


def far_sums(far_ref):
    senders, rows, _ = far_ref.shape
    total = far_ref[0, rows - EXTRA :, :].astype(jnp.float32)
    for s in range(1, senders):
        total += far_ref[s, rows - EXTRA :, :].astype(jnp.float32)
    return get_sums(total)


def middle_kernel(
    cols_ref, count_ref, far_ref, tiles_ref, panel_ref, x_ref,
    image_ref, z_ref, out_ref, sums_ref, total_ref, *, total_rows,
):
    copies, _, width = out_ref.shape
    per_dev, size, _ = x_ref.shape
    square_x, cross_x = far_sums(far_ref)
    guess = cross_x / (square_x + EPS * total_rows)
    sums_ref[0:1, :] = square_x
    sums_ref[1:2, :] = guess
    cross = jnp.zeros((1, width), jnp.float32)
    square = jnp.zeros((1, width), jnp.float32)
    for p in range(per_dev):
        image = row_image(cols_ref, count_ref, far_ref, tiles_ref, panel_ref, p, total_ref)
        image_ref[p] = image
        x = x_ref[p].astype(jnp.float32)
        moved = image - guess * x
        cross += jnp.sum(x * moved, axis=0, keepdims=True)
        square += jnp.sum(moved * moved, axis=0, keepdims=True)
        z = moved.astype(jnp.bfloat16)
        z_ref[p] = z
        for k in range(copies):
            out_ref[k, p * size : (p + 1) * size, :] = z
    extra = put_sums((cross, square), width)
    for k in range(copies):
        out_ref[k, per_dev * size :, :] = extra


def last_kernel(
    cols_ref, count_ref, far_ref, tiles_ref, panel_ref, x_ref, image_ref, sums_ref,
    basis_ref, out_ref, coef_ref, total_ref, *, total_rows,
):
    per_dev = x_ref.shape[0]
    cross, square = far_sums(far_ref)
    cross, square = cross / total_rows, square / total_rows
    mean_x = sums_ref[0:1, :] / total_rows
    guess = sums_ref[1:2, :]
    scale = lax.rsqrt(mean_x + EPS)
    proj = scale * scale * (cross + guess * mean_x)
    off = proj - guess
    mean_rest = scale * scale * (square - 2.0 * off * cross + off * off * mean_x)
    mean_rest = jnp.maximum(mean_rest, 0.0) + EPS
    factor = scale * lax.rsqrt(mean_rest)
    coef_ref[0:1, :] = proj
    coef_ref[1:2, :] = jnp.sqrt(mean_rest)
    for p in range(per_dev):
        image = image_ref[p]
        x = x_ref[p].astype(jnp.float32)
        basis_ref[p] = ((image - guess * x - off * x) * factor).astype(jnp.bfloat16)
        second = row_image(cols_ref, count_ref, far_ref, tiles_ref, panel_ref, p, total_ref)
        out_ref[p] = (second - off * image) * factor


def body(rhs_block, far_u, far_w, far_ranks, near_tiles, near_cols, near_count):
    panel_count = lax.axis_size("blk")
    slice_count = lax.axis_size("near")
    my_panel = lax.axis_index("blk")
    my_slice = lax.axis_index("near")
    per_dev, size, width = rhs_block.shape[1:]
    total_rows = float(per_dev * size * panel_count * slice_count)
    slots = near_cols.shape[2]
    targets = far_u.shape[0]
    rank = far_u.shape[3]
    zs = panel_count // 4
    rows = per_dev * size + EXTRA
    bf16, f32 = jnp.bfloat16, jnp.float32

    x = rhs_block[0]
    tiles = near_tiles[0]
    place = jnp.stack([my_panel // (2 * zs), my_panel % 2]).astype(jnp.int32)
    slot_live = jnp.arange(slots, dtype=jnp.int32)[None, :] < near_count[0][:, None]
    mine = my_slice * per_dev + jnp.arange(per_dev, dtype=jnp.int32)
    is_near = jnp.any((near_cols[0][:, :, None] == mine) & slot_live[:, :, None], axis=1)
    same = jnp.arange(panel_count, dtype=jnp.int32) == my_panel
    near_pair = same[:, None, None] & is_near.T[None]
    ranks = jnp.where(near_pair, 0, far_ranks.transpose(1, 2, 0)).reshape(-1, targets)
    my_cols = lax.dynamic_slice_in_dim(near_cols[0], my_slice * per_dev, per_dev, 0)
    my_count = lax.dynamic_slice_in_dim(near_count[0], my_slice * per_dev, per_dev, 0)

    z_groups = [[h * 2 * zs + z * 2 + c for z in range(zs)] for h in range(2) for c in range(2)]
    flip_x = [(i, (i + 2 * zs) % panel_count) for i in range(panel_count)]
    flip_core = [(i, i ^ 1) for i in range(panel_count)]

    def gather_panels(payload):
        crossed = lax.ppermute(payload[0], "blk", flip_x)
        here = lax.all_to_all(payload, "blk", 0, 0, tiled=True, axis_index_groups=z_groups)
        here_other = lax.ppermute(here, "blk", flip_core)
        crossed = jnp.broadcast_to(crossed[None], payload.shape)
        there = lax.all_to_all(crossed, "blk", 0, 0, tiled=True, axis_index_groups=z_groups)
        there_other = lax.ppermute(there, "blk", flip_core)
        return here, there, here_other, there_other

    def far_products(gathered):
        half = 2 * zs
        own = lambda j, *_: (jnp.minimum(j, zs - 1), 0, 0)
        far = lambda j, *_: (jnp.clip(j - zs, 0, zs - 1), 0, 0)

        def w_block(j, place_ref, rank_ref):
            j = jnp.minimum(j, half - 1)
            side = j // zs
            xh = place_ref[0]
            return (0, jnp.where(side == 1, 1 - xh, xh) * zs + j % zs, 0, 0, 0)

        last = lambda j, *_: (jnp.maximum(j - half, 0), 0, 0)
        u_block = lambda j, *_: (jnp.maximum(j - half, 0), 0, 0, 0, 0)
        return pl.pallas_call(
            functools.partial(
                far_kernel, zs=zs, per_dev=per_dev, targets=targets, rank=rank, size=size
            ),
            out_shape=jax.ShapeDtypeStruct((slice_count, rows, width), bf16),
            grid_spec=pltpu.PrefetchScalarGridSpec(
                num_scalar_prefetch=2,
                grid=(half + slice_count,),
                in_specs=[
                    pl.BlockSpec((targets, 2, per_dev, rank, size), w_block),
                    pl.BlockSpec((per_dev, panel_count, per_dev, rank, size), u_block),
                    pl.BlockSpec((1, rows, width), own),
                    pl.BlockSpec((1, rows, width), far),
                    pl.BlockSpec((1, rows, width), own),
                    pl.BlockSpec((1, rows, width), far),
                ],
                out_specs=pl.BlockSpec((1, rows, width), last),
                scratch_shapes=[
                    pltpu.VMEM((targets, panel_count, per_dev * rank, width), bf16),
                    pltpu.VMEM((EXTRA, width), f32),
                ],
            ),
            compiler_params=pltpu.CompilerParams(vmem_limit_bytes=40 * MIB),
            cost_estimate=pl.CostEstimate(
                flops=4 * targets * panel_count * per_dev * rank * size * width,
                bytes_accessed=24 * MIB,
                transcendentals=0,
            ),
        )(place, ranks, far_w, far_u, *gathered)

    def scatter_panel(parts):
        return lax.all_to_all(parts, "near", 0, 0, tiled=True)

    smem = pl.BlockSpec(memory_space=pltpu.SMEM)
    vmem = pl.BlockSpec(memory_space=pltpu.VMEM)
    params = pltpu.CompilerParams(vmem_limit_bytes=40 * MIB)
    work = [pltpu.VMEM((size, width), f32)]

    payload = pl.pallas_call(
        start_kernel,
        grid=(1,),
        out_shape=jax.ShapeDtypeStruct((zs, rows, width), bf16),
        in_specs=[whole(x.shape), whole((per_dev, 1, size, size))],
        out_specs=whole((zs, rows, width)),
        compiler_params=params,
    )(x, tiles)
    panel_x = lax.all_gather(x, "near", axis=0, tiled=True)
    far_x = scatter_panel(far_products(gather_panels(payload)))
    image, z, payload, sums = pl.pallas_call(
        functools.partial(middle_kernel, total_rows=total_rows),
        out_shape=(
            jax.ShapeDtypeStruct((per_dev, size, width), f32),
            jax.ShapeDtypeStruct((per_dev, size, width), bf16),
            jax.ShapeDtypeStruct((zs, rows, width), bf16),
            jax.ShapeDtypeStruct((2, width), f32),
        ),
        in_specs=[smem, smem, vmem, vmem, vmem, vmem],
        out_specs=(vmem, vmem, vmem, vmem),
        scratch_shapes=work,
        compiler_params=params,
    )(my_cols, my_count, far_x, tiles, panel_x, x)
    panel_z = lax.all_gather(z, "near", axis=0, tiled=True)
    far_z = scatter_panel(far_products(gather_panels(payload)))
    second_basis, second_image, coefficients = pl.pallas_call(
        functools.partial(last_kernel, total_rows=total_rows),
        out_shape=(
            jax.ShapeDtypeStruct((per_dev, size, width), bf16),
            jax.ShapeDtypeStruct((per_dev, size, width), f32),
            jax.ShapeDtypeStruct((2, width), f32),
        ),
        in_specs=[smem, smem, vmem, vmem, vmem, vmem, vmem, vmem],
        out_specs=(vmem, vmem, vmem),
        scratch_shapes=work,
        compiler_params=params,
    )(my_cols, my_count, far_z, tiles, panel_z, x, image, sums)
    return second_basis[None], second_image[None], coefficients


def solution(mesh):
    placed = (
        P("blk", "near", None, None),
        P("blk", None, "near", None, None),
        P("blk", None, "near", None, None),
        P("blk", None, "near"),
        P("blk", "near", None, None, None),
        P("blk", None, None),
        P("blk", None),
    )
    return jax.shard_map(
        body,
        mesh=mesh,
        in_specs=placed,
        out_specs=(P("blk", "near", None, None), P("blk", "near", None, None), P()),
        check_vma=False,
    )
```

```python
import functools

import jax
import jax.numpy as jnp
from jax import lax
from jax.experimental import pallas as pl
from jax.experimental.pallas import tpu as pltpu
from jax.sharding import PartitionSpec as P

EPS = 1e-06
EXTRA = 16
MIB = 1 << 20


def put_sums(sums, width):
    rows = []
    for value in sums:
        high = value.astype(jnp.bfloat16)
        left = value - high.astype(jnp.float32)
        middle = left.astype(jnp.bfloat16)
        low = (left - middle.astype(jnp.float32)).astype(jnp.bfloat16)
        rows += [high, middle, low]
    rows.append(jnp.zeros((EXTRA - len(rows), width), jnp.bfloat16))
    return jnp.concatenate(rows, axis=0)


def get_sums(rows):
    return (
        rows[0:1] + rows[1:2] + rows[2:3],
        rows[3:4] + rows[4:5] + rows[5:6],
    )


def whole(shape):
    return pl.BlockSpec(shape, lambda *_: (0,) * len(shape))


def start_kernel(x_ref, own_ref, out_ref):
    per_dev, size, width = x_ref.shape
    square = jnp.zeros((1, width), jnp.float32)
    cross = jnp.zeros((1, width), jnp.float32)
    for p in range(per_dev):
        x = x_ref[p]
        x_f = x.astype(jnp.float32)
        image = jnp.dot(own_ref[p, 0], x, preferred_element_type=jnp.float32)
        square += jnp.sum(x_f * x_f, axis=0, keepdims=True)
        cross += jnp.sum(x_f * image, axis=0, keepdims=True)
        out_ref[p * size : (p + 1) * size, :] = x
    out_ref[per_dev * size :, :] = put_sums((square, cross), width)


def load_kernel(w_ref, u_ref, held_w, held_u, done_ref, w_sem, u_sem):
    copies = []
    for source, target, sems in ((w_ref, held_w, w_sem), (u_ref, held_u, u_sem)):
        copies += [
            pltpu.make_async_copy(source.at[k], target.at[k], sems.at[k])
            for k in range(source.shape[0])
        ]
    for copy in copies:
        copy.start()
    for copy in copies:
        copy.wait()
    done_ref[...] = jnp.zeros_like(done_ref)


def pack_kernel(*refs):
    count = len(refs) - 3
    _, out_ref, sems = refs[count:]
    copies = [
        pltpu.make_async_copy(refs[n], out_ref.at[n], sems.at[n]) for n in range(count)
    ]
    for copy in copies:
        copy.start()
    for copy in copies:
        copy.wait()


class Coder:
    def __init__(self, first, order_ref, rank_ref, w_ref, fields, field_buf, field_sem):
        self.first, self.order_ref, self.rank_ref = first, order_ref, rank_ref
        self.w_ref, self.field_buf = w_ref, field_buf
        parts = [field.at[n] for field in fields for n in range(field.shape[0])]
        self.copies = [
            pltpu.make_async_copy(part, field_buf.at[slot], field_sem.at[slot])
            for slot, part in enumerate(parts)
        ]

    def load(self):
        for copy in self.copies:
            copy.start()

    def run(self, coded_ref, sums_ref, by_panel):
        targets, _, per_dev, rank, size = self.w_ref.shape
        width = coded_ref.shape[3]
        row = lax.broadcasted_iota(jnp.int32, (rank, width), 0)
        for slot, copy in enumerate(self.copies):
            panel = self.order_ref[self.first + slot]
            place = panel if by_panel else slot
            copy.wait()
            sums_ref[...] += self.field_buf[slot, per_dev * size :, :].astype(jnp.float32)
            for p in range(per_dev):
                w = self.w_ref[:, panel, p].reshape(targets * rank, size)
                field = self.field_buf[slot, p * size : (p + 1) * size, :]
                value = jnp.dot(w, field, preferred_element_type=jnp.float32)
                for i in range(targets):
                    live = self.rank_ref[panel * per_dev + p, i]
                    part = value[i * rank : (i + 1) * rank]
                    part = jnp.where(row < live, part, 0.0).astype(jnp.bfloat16)
                    coded_ref[i, place, p * rank : (p + 1) * rank, :] = part


def code_kernel(order_ref, rank_ref, w_ref, *refs):
    fields, (coded_ref, sums_ref, field_buf, field_sem) = refs[:-4], refs[-4:]
    coder = Coder(0, order_ref, rank_ref, w_ref, fields, field_buf, field_sem)
    coder.load()
    sums_ref[...] = jnp.zeros_like(sums_ref)
    coder.run(coded_ref, sums_ref, False)


def far_kernel(order_ref, rank_ref, w_ref, u_ref, early_ref, early_sums_ref, *refs):
    fields, refs = refs[:-8], refs[-8:]
    out_ref, field_buf, coded_ref, out_buf, sums_ref, field_sem, early_sem, out_sem = refs
    receivers, rows, width = out_ref.shape
    _, _, per_dev, _, size = u_ref.shape
    blocks = per_dev * size
    early = early_ref.shape[1]

    def early_copy(slot):
        return pltpu.make_async_copy(
            early_ref.at[:, slot], coded_ref.at[:, order_ref[slot]], early_sem.at[slot]
        )

    def out_copy(j):
        return pltpu.make_async_copy(out_buf.at[j], out_ref.at[j], out_sem.at[j])

    coder = Coder(early, order_ref, rank_ref, w_ref, fields, field_buf, field_sem)
    coder.load()
    for slot in range(early):
        early_copy(slot).start()
    sums_ref[...] = early_sums_ref[...]
    coder.run(coded_ref, sums_ref, True)
    extra = put_sums(get_sums(sums_ref[...]), width)
    for slot in range(early):
        early_copy(slot).wait()

    def expand(j, carry):
        for p in range(per_dev):
            u = u_ref[per_dev * j + p].reshape(-1, size)
            value = coded_ref[per_dev * j + p].reshape(-1, width)
            total = lax.dot_general(
                u, value, (((0,), (0,)), ((), ())), preferred_element_type=jnp.float32
            )
            out_buf[j, p * size : (p + 1) * size, :] = total.astype(jnp.bfloat16)
        out_buf[j, blocks:, :] = extra
        out_copy(j).start()
        return carry

    lax.fori_loop(0, receivers, expand, 0)
    for j in range(receivers):
        out_copy(j).wait()


def near_kernel(cols_ref, count_ref, tiles_ref, panel_ref, out_ref, panel_buf, tile_buf, sems):
    per_dev = out_ref.shape[0]
    copies = [pltpu.make_async_copy(panel_ref, panel_buf, sems.at[per_dev])]
    copies += [
        pltpu.make_async_copy(tiles_ref.at[p], tile_buf.at[p], sems.at[p]) for p in range(per_dev)
    ]
    for copy in copies:
        copy.start()
    for copy in copies:
        copy.wait()
    for p in range(per_dev):
        out_ref[p] = jnp.zeros(out_ref.shape[1:], jnp.float32)
        for k in range(tile_buf.shape[1]):

            @pl.when(k < count_ref[p])
            def _():
                out_ref[p] += jnp.dot(
                    tile_buf[p, k], panel_buf[cols_ref[p, k]], preferred_element_type=jnp.float32
                )


class FarTotal:
    def __init__(self, far_ref, buf, sems):
        self.buf = buf
        self.copies = [
            pltpu.make_async_copy(far_ref.at[s], buf.at[s], sems.at[s])
            for s in range(buf.shape[0])
        ]
        for copy in self.copies:
            copy.start()

    def wait(self):
        for copy in self.copies:
            copy.wait()

    def rows(self, start, stop):
        total = self.buf[0, start:stop, :].astype(jnp.float32)
        for s in range(1, self.buf.shape[0]):
            total += self.buf[s, start:stop, :].astype(jnp.float32)
        return total

    def sums(self):
        rows = self.buf.shape[1]
        return get_sums(self.rows(rows - EXTRA, rows))


def middle_kernel(
    far_ref, near_ref, x_ref, image_ref, sums_ref, z_ref, out_ref, far_buf, far_sem, *, total_rows
):
    per_dev, size, width = x_ref.shape
    far = FarTotal(far_ref, far_buf, far_sem)
    far.wait()
    square_x, cross_x = far.sums()
    guess = cross_x / (square_x + EPS * total_rows)
    sums_ref[0:1, :] = square_x
    sums_ref[1:2, :] = guess
    cross = jnp.zeros((1, width), jnp.float32)
    square = jnp.zeros((1, width), jnp.float32)
    for p in range(per_dev):
        image = far.rows(p * size, (p + 1) * size) + near_ref[p]
        image_ref[p] = image
        x = x_ref[p].astype(jnp.float32)
        moved = image - guess * x
        cross += jnp.sum(x * moved, axis=0, keepdims=True)
        square += jnp.sum(moved * moved, axis=0, keepdims=True)
        z = moved.astype(jnp.bfloat16)
        z_ref[p] = z
        out_ref[p * size : (p + 1) * size, :] = z
    out_ref[per_dev * size :, :] = put_sums((cross, square), width)


def last_kernel(
    far_ref, near_ref, x_ref, image_ref, sums_ref, basis_ref, out_ref, coef_ref, far_buf, far_sem,
    *, total_rows,
):
    per_dev, size, _ = x_ref.shape
    far = FarTotal(far_ref, far_buf, far_sem)
    far.wait()
    cross, square = far.sums()
    cross, square = cross / total_rows, square / total_rows
    mean_x = sums_ref[0:1, :] / total_rows
    guess = sums_ref[1:2, :]
    scale = lax.rsqrt(mean_x + EPS)
    proj = scale * scale * (cross + guess * mean_x)
    off = proj - guess
    mean_rest = scale * scale * (square - 2.0 * off * cross + off * off * mean_x)
    mean_rest = jnp.maximum(mean_rest, 0.0) + EPS
    factor = scale * lax.rsqrt(mean_rest)
    coef_ref[0:1, :] = proj
    coef_ref[1:2, :] = jnp.sqrt(mean_rest)
    for p in range(per_dev):
        image = image_ref[p]
        x = x_ref[p].astype(jnp.float32)
        basis_ref[p] = ((image - guess * x - off * x) * factor).astype(jnp.bfloat16)
        second = far.rows(p * size, (p + 1) * size) + near_ref[p]
        out_ref[p] = (second - off * image) * factor


def body(rhs_block, far_u, far_w, far_ranks, near_tiles, near_cols, near_count):
    panel_count = lax.axis_size("blk")
    slice_count = lax.axis_size("near")
    my_panel = lax.axis_index("blk")
    my_slice = lax.axis_index("near")
    per_dev, size, width = rhs_block.shape[1:]
    total_rows = float(per_dev * size * panel_count * slice_count)
    slots = near_cols.shape[2]
    targets = far_u.shape[0]
    rank = far_u.shape[3]
    chips = panel_count // 2
    rows = per_dev * size + EXTRA
    bf16, f32, i32 = jnp.bfloat16, jnp.float32, jnp.int32

    x = rhs_block[0]
    tiles = near_tiles[0]
    slot_live = jnp.arange(slots, dtype=i32)[None, :] < near_count[0][:, None]
    mine = my_slice * per_dev + jnp.arange(per_dev, dtype=i32)
    is_near = jnp.any((near_cols[0][:, :, None] == mine) & slot_live[:, :, None], axis=1)
    same = jnp.arange(panel_count, dtype=i32) == my_panel
    near_pair = same[:, None, None] & is_near.T[None]
    ranks = jnp.where(near_pair, 0, far_ranks.transpose(1, 2, 0)).reshape(-1, targets)
    my_cols = lax.dynamic_slice_in_dim(near_cols[0], my_slice * per_dev, per_dev, 0)
    my_count = lax.dynamic_slice_in_dim(near_count[0], my_slice * per_dev, per_dev, 0)

    hbm = pl.BlockSpec(memory_space=pltpu.HBM)
    smem = pl.BlockSpec(memory_space=pltpu.SMEM)
    vmem = pl.BlockSpec(memory_space=pltpu.VMEM)
    sems = pltpu.SemaphoreType.DMA
    in_hbm = pltpu.HBM

    def params(mib):
        return pltpu.CompilerParams(vmem_limit_bytes=mib * MIB)

    def cost(flops, mib):
        return pl.CostEstimate(flops=flops, bytes_accessed=mib * MIB, transcendentals=0)

    zs = chips // 2
    z_turns = (0, 1, 3, 2)

    def along_z(turn):
        return [
            (i, i // chips * chips + ((i // 2 - turn) % zs) * 2 + i % 2) for i in range(panel_count)
        ]

    flip_core = [(i, i ^ 1) for i in range(panel_count)]
    flip_far = [(i, (i + chips) % panel_count) for i in range(panel_count)]
    core = my_panel % 2
    near_z = [
        my_panel // chips * chips + 2 * ((my_panel // 2 + turn) % zs) for turn in z_turns
    ]
    far_z = [(at + chips) % panel_count for at in near_z]
    first = near_z[:1] + far_z[:1] + near_z[1:] + far_z[1:]
    order = jnp.stack(
        [at + core for at in first] + [at + 1 - core for at in first]
    ).astype(i32)

    def pack(blocks, loaded):
        count = len(blocks)
        return pl.pallas_call(
            pack_kernel,
            out_shape=jax.ShapeDtypeStruct((count, rows, width), bf16),
            in_specs=[hbm] * count + [vmem],
            out_specs=hbm,
            scratch_shapes=[sems((count,))],
            compiler_params=params(1),
        )(*blocks, loaded)

    def gather_panels(payload, loaded):
        far = lax.ppermute(payload, "blk", flip_far)
        own = [lax.ppermute(payload, "blk", along_z(turn)) for turn in z_turns[1:]]
        late = [lax.ppermute(far, "blk", along_z(turn)) for turn in z_turns[1:]]
        own = pack([payload, far] + own + late, loaded)
        return [own], [lax.ppermute(own, "blk", flip_core)]

    flops = 2 * targets * panel_count * per_dev * rank * size * width

    def coder_scratch(n):
        return [pltpu.VMEM((n, rows, width), bf16)]

    far_w, order, ranks, my_cols, my_count = lax.optimization_barrier(
        (far_w, order, ranks, my_cols, my_count)
    )

    def load_factors(far_w, far_u):
        return pl.pallas_call(
            load_kernel,
            out_shape=(
                pltpu.VMEM(far_w.shape, bf16),
                pltpu.VMEM(far_u.shape, bf16),
                jax.ShapeDtypeStruct((8, 128), f32),
            ),
            in_specs=[hbm, hbm],
            out_specs=(vmem, vmem, vmem),
            scratch_shapes=[sems((targets,)), sems((targets,))],
            compiler_params=params(44),
            cost_estimate=cost(0, 32),
        )(far_w, far_u)

    def far_products(payload, far_w, far_u):
        held_w, held_u, loaded = load_factors(far_w, far_u)
        early, late = gather_panels(payload, loaded)
        n = sum(field.shape[0] for field in early)
        m = panel_count - n
        coded, sums = pl.pallas_call(
            code_kernel,
            out_shape=(
                pltpu.VMEM((targets, n, per_dev * rank, width), bf16),
                jax.ShapeDtypeStruct((EXTRA, width), f32),
            ),
            in_specs=[smem, smem, vmem] + [hbm] * len(early),
            out_specs=(vmem, vmem),
            scratch_shapes=coder_scratch(n) + [sems((n,))],
            compiler_params=params(8),
            cost_estimate=cost(flops * n // panel_count, 16),
        )(order, ranks, held_w, *early)
        return pl.pallas_call(
            far_kernel,
            out_shape=in_hbm((slice_count, rows, width), bf16),
            in_specs=[smem, smem, vmem, vmem, hbm, vmem] + [hbm] * len(late),
            out_specs=hbm,
            scratch_shapes=coder_scratch(m)
            + [
                pltpu.VMEM((targets, panel_count, per_dev * rank, width), bf16),
                pltpu.VMEM((slice_count, rows, width), bf16),
                pltpu.VMEM((EXTRA, width), f32),
            ]
            + [sems((m,)), sems((n,)), sems((slice_count,))],
            compiler_params=params(18),
            cost_estimate=cost(flops + flops * m // panel_count, 20),
        )(order, ranks, held_w, held_u, coded, sums, *late)

    def near_products(panel):
        return pl.pallas_call(
            near_kernel,
            out_shape=jax.ShapeDtypeStruct((per_dev, size, width), f32),
            in_specs=[smem, smem, hbm, hbm],
            out_specs=vmem,
            scratch_shapes=[
                pltpu.VMEM((slice_count * per_dev, size, width), bf16),
                pltpu.VMEM((per_dev, slots, size, size), bf16),
                sems((per_dev + 1,)),
            ],
            compiler_params=params(10),
            cost_estimate=cost(2 * per_dev * slots * size * size * width, 5),
        )(my_cols, my_count, tiles, panel)

    def gather_near(blocks):
        return lax.all_gather(blocks, "near", axis=0, tiled=True)

    def scatter_panel(parts, panel):
        parts, panel = lax.optimization_barrier((parts, panel))
        return lax.all_to_all(parts, "near", 0, 0, tiled=True), panel

    payload = pl.pallas_call(
        start_kernel,
        grid=(1,),
        out_shape=jax.ShapeDtypeStruct((rows, width), bf16),
        in_specs=[whole(x.shape), whole((per_dev, 1, size, size))],
        out_specs=whole((rows, width)),
        compiler_params=params(60),
    )(x, tiles)
    panel = gather_near(x)
    far_x, panel = scatter_panel(far_products(payload, far_w, far_u), panel)
    far_scratch = [pltpu.VMEM((slice_count, rows, width), bf16), sems((slice_count,))]
    image, sums, z, payload = pl.pallas_call(
        functools.partial(middle_kernel, total_rows=total_rows),
        out_shape=(
            jax.ShapeDtypeStruct((per_dev, size, width), f32),
            jax.ShapeDtypeStruct((2, width), f32),
            in_hbm((per_dev, size, width), bf16),
            jax.ShapeDtypeStruct((rows, width), bf16),
        ),
        in_specs=[hbm, vmem, vmem],
        out_specs=(vmem,) * 4,
        scratch_shapes=far_scratch,
        compiler_params=params(8),
    )(far_x, near_products(panel), x)
    panel = gather_near(z)
    payload, far_w, far_u = lax.optimization_barrier((payload, far_w, far_u))
    far_z, panel = scatter_panel(far_products(payload, far_w, far_u), panel)
    second_basis, second_image, coefficients = pl.pallas_call(
        functools.partial(last_kernel, total_rows=total_rows),
        out_shape=(
            jax.ShapeDtypeStruct((per_dev, size, width), bf16),
            jax.ShapeDtypeStruct((per_dev, size, width), f32),
            jax.ShapeDtypeStruct((2, width), f32),
        ),
        in_specs=[hbm, vmem, vmem, vmem, vmem],
        out_specs=(vmem, vmem, vmem),
        scratch_shapes=far_scratch,
        compiler_params=params(8),
    )(far_z, near_products(panel), x, image, sums)
    return second_basis[None], second_image[None], coefficients


def solution(mesh):
    placed = (
        P("blk", "near", None, None),
        P("blk", None, "near", None, None),
        P("blk", None, "near", None, None),
        P("blk", None, "near"),
        P("blk", "near", None, None, None),
        P("blk", None, None),
        P("blk", None),
    )
    return jax.shard_map(
        body,
        mesh=mesh,
        in_specs=placed,
        out_specs=(P("blk", "near", None, None), P("blk", "near", None, None), P()),
        check_vma=False,
    )
```

```python
import functools

import jax
import jax.numpy as jnp
from jax import lax
from jax.experimental import pallas as pl
from jax.experimental.pallas import tpu as pltpu
from jax.sharding import PartitionSpec as P

EPS = 1e-06
EXTRA = 16
MIB = 1 << 20


def put_sums(sums, width):
    rows = []
    for value in sums:
        high = value.astype(jnp.bfloat16)
        left = value - high.astype(jnp.float32)
        middle = left.astype(jnp.bfloat16)
        low = (left - middle.astype(jnp.float32)).astype(jnp.bfloat16)
        rows += [high, middle, low]
    rows.append(jnp.zeros((EXTRA - len(rows), width), jnp.bfloat16))
    return jnp.concatenate(rows, axis=0)


def get_sums(rows):
    return (
        rows[0:1] + rows[1:2] + rows[2:3],
        rows[3:4] + rows[4:5] + rows[5:6],
    )


def whole(shape):
    return pl.BlockSpec(shape, lambda *_: (0,) * len(shape))


def start_kernel(x_ref, own_ref, out_ref):
    per_dev, size, width = x_ref.shape
    square = jnp.zeros((1, width), jnp.float32)
    cross = jnp.zeros((1, width), jnp.float32)
    for p in range(per_dev):
        x = x_ref[p]
        x_f = x.astype(jnp.float32)
        image = jnp.dot(own_ref[p, 0], x, preferred_element_type=jnp.float32)
        square += jnp.sum(x_f * x_f, axis=0, keepdims=True)
        cross += jnp.sum(x_f * image, axis=0, keepdims=True)
        out_ref[p * size : (p + 1) * size, :] = x
    out_ref[per_dev * size :, :] = put_sums((square, cross), width)


def load_kernel(w_ref, u_ref, held_w, held_u, w_sem, u_sem):
    copies = []
    for source, target, sems in ((w_ref, held_w, w_sem), (u_ref, held_u, u_sem)):
        copies += [
            pltpu.make_async_copy(source.at[k], target.at[k], sems.at[k])
            for k in range(source.shape[0])
        ]
    for copy in copies:
        copy.start()
    for copy in copies:
        copy.wait()


def pack_kernel(*refs):
    count = len(refs) - 3
    _, out_ref, sems = refs[count:]
    copies = [
        pltpu.make_async_copy(refs[n], out_ref.at[n], sems.at[n]) for n in range(count)
    ]
    for copy in copies:
        copy.start()
    for copy in copies:
        copy.wait()


class Coder:
    def __init__(self, first, order_ref, rank_ref, w_ref, fields, field_buf, field_sem):
        self.first, self.order_ref, self.rank_ref = first, order_ref, rank_ref
        self.w_ref, self.field_buf = w_ref, field_buf
        parts = [field.at[n] for field in fields for n in range(field.shape[0])]
        self.copies = [
            pltpu.make_async_copy(part, field_buf.at[slot], field_sem.at[slot])
            for slot, part in enumerate(parts)
        ]

    def load(self):
        for copy in self.copies:
            copy.start()

    def run(self, coded_ref, sums_ref, by_panel):
        targets, _, per_dev, rank, size = self.w_ref.shape
        width = coded_ref.shape[3]
        row = lax.broadcasted_iota(jnp.int32, (rank, width), 0)
        for slot, copy in enumerate(self.copies):
            panel = self.order_ref[self.first + slot]
            place = panel if by_panel else slot
            copy.wait()
            sums_ref[...] += self.field_buf[slot, per_dev * size :, :].astype(jnp.float32)
            for p in range(per_dev):
                w = self.w_ref[:, panel, p].reshape(targets * rank, size)
                field = self.field_buf[slot, p * size : (p + 1) * size, :]
                value = jnp.dot(w, field, preferred_element_type=jnp.float32)
                for i in range(targets):
                    live = self.rank_ref[panel * per_dev + p, i]
                    part = value[i * rank : (i + 1) * rank]
                    part = jnp.where(row < live, part, 0.0).astype(jnp.bfloat16)
                    coded_ref[i, place, p * rank : (p + 1) * rank, :] = part


def code_kernel(order_ref, rank_ref, w_ref, *refs):
    fields, (coded_ref, sums_ref, field_buf, field_sem) = refs[:-4], refs[-4:]
    coder = Coder(0, order_ref, rank_ref, w_ref, fields, field_buf, field_sem)
    coder.load()
    sums_ref[...] = jnp.zeros_like(sums_ref)
    coder.run(coded_ref, sums_ref, False)


def far_kernel(order_ref, rank_ref, target_ref, w_ref, u_ref, early_ref, early_sums_ref, *refs):
    fields, refs = refs[:-11], refs[-11:]
    cross_ref, stay_ref, around_refs, near_ref = refs[0], refs[1], refs[2:5], refs[5]
    field_buf, coded_ref, sums_ref, field_sem, early_sem = refs[6:]
    turns = cross_ref.shape[0]
    width = cross_ref.shape[2]
    _, _, per_dev, _, size = u_ref.shape
    early = early_ref.shape[1]

    def early_copy(slot):
        return pltpu.make_async_copy(
            early_ref.at[:, slot], coded_ref.at[:, order_ref[slot]], early_sem.at[slot]
        )

    coder = Coder(early, order_ref, rank_ref, w_ref, fields, field_buf, field_sem)
    coder.load()
    for slot in range(early):
        early_copy(slot).start()
    sums_ref[...] = early_sums_ref[...]
    coder.run(coded_ref, sums_ref, True)
    extra = put_sums(get_sums(sums_ref[...]), width)
    for slot in range(early):
        early_copy(slot).wait()

    def expand(target):
        u = u_ref[target].reshape(-1, size)
        value = coded_ref[target].reshape(-1, width)
        total = lax.dot_general(
            u, value, (((0,), (0,)), ((), ())), preferred_element_type=jnp.float32
        )
        return total.astype(jnp.bfloat16)

    for turn in range(turns):
        around_ref = near_ref if turn == 0 else around_refs[turn - 1]
        for side, first_ref in ((1, cross_ref), (0, stay_ref)):
            target = target_ref[side * turns + turn] * per_dev
            first_ref[turn] = expand(target)
            around_ref[side * size : (side + 1) * size, :] = expand(target + 1)
        around_ref[2 * size :, :] = extra


def add_kernel(
    stay_ref, cross_ref, near_ref, a1_ref, a2_ref, a3_ref,
    first_ref, s1_ref, s2_ref, s3_ref, second_ref, send_ref, sums_ref,
):
    size = stay_ref.shape[1]
    for turn, out_ref in enumerate((first_ref, s1_ref, s2_ref, s3_ref)):
        total = stay_ref[turn].astype(jnp.float32) + cross_ref[turn].astype(jnp.float32)
        out_ref[...] = total.astype(out_ref.dtype)

    def rows(start, stop):
        total = near_ref[start:stop, :].astype(jnp.float32)
        for ref in (a1_ref, a2_ref, a3_ref):
            total += ref[start:stop, :].astype(jnp.float32)
        return total

    second_ref[...] = rows(0, size)
    send_ref[:size, :] = rows(size, 2 * size).astype(jnp.bfloat16)
    sums = get_sums(rows(2 * size, 2 * size + EXTRA))
    send_ref[size:, :] = put_sums(sums, send_ref.shape[1])
    sums_ref[0:1, :], sums_ref[1:2, :] = sums


def near_kernel(cols_ref, count_ref, tiles_ref, panel_ref, out_ref, panel_buf, tile_buf, sems):
    per_dev = out_ref.shape[0]
    copies = [pltpu.make_async_copy(panel_ref, panel_buf, sems.at[per_dev])]
    copies += [
        pltpu.make_async_copy(tiles_ref.at[p], tile_buf.at[p], sems.at[p]) for p in range(per_dev)
    ]
    for copy in copies:
        copy.start()
    for copy in copies:
        copy.wait()
    for p in range(per_dev):
        out_ref[p] = jnp.zeros(out_ref.shape[1:], jnp.float32)
        for k in range(tile_buf.shape[1]):

            @pl.when(k < count_ref[p])
            def _():
                out_ref[p] += jnp.dot(
                    tile_buf[p, k], panel_buf[cols_ref[p, k]], preferred_element_type=jnp.float32
                )


class FarTotal:
    def __init__(self, first_ref, r1_ref, r2_ref, r3_ref, second_ref, cross_ref, sums_ref):
        self.blocks = ((first_ref, r1_ref, r2_ref, r3_ref), (second_ref, cross_ref))
        self.sums_ref = sums_ref

    def block(self, p):
        total, *others = self.blocks[p]
        size = total.shape[0]
        total = total[...]
        for ref in others:
            total += ref[:size, :].astype(jnp.float32)
        return total

    def sums(self):
        cross_ref = self.blocks[1][1]
        size = cross_ref.shape[0] - EXTRA
        came = get_sums(cross_ref[size:, :].astype(jnp.float32))
        return self.sums_ref[0:1, :] + came[0], self.sums_ref[1:2, :] + came[1]


def middle_kernel(*refs, total_rows):
    near_ref, x_ref, image_ref, sums_ref, z_ref, out_ref = refs[7:]
    per_dev, size, width = x_ref.shape
    far = FarTotal(*refs[:7])
    square_x, cross_x = far.sums()
    guess = cross_x / (square_x + EPS * total_rows)
    sums_ref[0:1, :] = square_x
    sums_ref[1:2, :] = guess
    cross = jnp.zeros((1, width), jnp.float32)
    square = jnp.zeros((1, width), jnp.float32)
    for p in range(per_dev):
        image = far.block(p) + near_ref[p]
        image_ref[p] = image
        x = x_ref[p].astype(jnp.float32)
        moved = image - guess * x
        cross += jnp.sum(x * moved, axis=0, keepdims=True)
        square += jnp.sum(moved * moved, axis=0, keepdims=True)
        z = moved.astype(jnp.bfloat16)
        z_ref[p] = z
        out_ref[p * size : (p + 1) * size, :] = z
    out_ref[per_dev * size :, :] = put_sums((cross, square), width)


def last_kernel(*refs, total_rows):
    near_ref, x_ref, image_ref, scale_ref, basis_ref, out_ref, coef_ref = refs[7:]
    per_dev = x_ref.shape[0]
    far = FarTotal(*refs[:7])
    cross, square = far.sums()
    cross, square = cross / total_rows, square / total_rows
    mean_x = scale_ref[0:1, :] / total_rows
    guess = scale_ref[1:2, :]
    scale = lax.rsqrt(mean_x + EPS)
    proj = scale * scale * (cross + guess * mean_x)
    off = proj - guess
    mean_rest = scale * scale * (square - 2.0 * off * cross + off * off * mean_x)
    mean_rest = jnp.maximum(mean_rest, 0.0) + EPS
    factor = scale * lax.rsqrt(mean_rest)
    coef_ref[0:1, :] = proj
    coef_ref[1:2, :] = jnp.sqrt(mean_rest)
    for p in range(per_dev):
        image = image_ref[p]
        x = x_ref[p].astype(jnp.float32)
        basis_ref[p] = ((image - guess * x - off * x) * factor).astype(jnp.bfloat16)
        second = far.block(p) + near_ref[p]
        out_ref[p] = (second - off * image) * factor


def body(rhs_block, far_u, far_w, far_ranks, near_tiles, near_cols, near_count):
    panel_count = lax.axis_size("blk")
    slice_count = lax.axis_size("near")
    my_panel = lax.axis_index("blk")
    my_slice = lax.axis_index("near")
    per_dev, size, width = rhs_block.shape[1:]
    total_rows = float(per_dev * size * panel_count * slice_count)
    slots = near_cols.shape[2]
    targets = far_u.shape[0]
    rank = far_u.shape[3]
    chips = panel_count // 2
    rows = per_dev * size + EXTRA
    bf16, f32, i32 = jnp.bfloat16, jnp.float32, jnp.int32

    x = rhs_block[0]
    tiles = near_tiles[0]
    slot_live = jnp.arange(slots, dtype=i32)[None, :] < near_count[0][:, None]
    mine = my_slice * per_dev + jnp.arange(per_dev, dtype=i32)
    is_near = jnp.any((near_cols[0][:, :, None] == mine) & slot_live[:, :, None], axis=1)
    same = jnp.arange(panel_count, dtype=i32) == my_panel
    near_pair = same[:, None, None] & is_near.T[None]
    ranks = jnp.where(near_pair, 0, far_ranks.transpose(1, 2, 0)).reshape(-1, targets)
    my_cols = lax.dynamic_slice_in_dim(near_cols[0], my_slice * per_dev, per_dev, 0)
    my_count = lax.dynamic_slice_in_dim(near_count[0], my_slice * per_dev, per_dev, 0)

    hbm = pl.BlockSpec(memory_space=pltpu.HBM)
    smem = pl.BlockSpec(memory_space=pltpu.SMEM)
    vmem = pl.BlockSpec(memory_space=pltpu.VMEM)
    sems = pltpu.SemaphoreType.DMA
    in_hbm = pltpu.HBM

    def params(mib):
        return pltpu.CompilerParams(vmem_limit_bytes=mib * MIB)

    def cost(flops, mib):
        return pl.CostEstimate(flops=flops, bytes_accessed=mib * MIB, transcendentals=0)

    zs = chips // 2
    ys = slice_count // 2
    my_x, my_y = my_slice // ys, my_slice % ys
    receivers = jnp.stack(
        [(my_x + side) % 2 * ys + (my_y + turn) % ys for side in range(2) for turn in range(ys)]
    ).astype(i32)
    flip_x = [(i, (i + ys) % slice_count) for i in range(slice_count)]

    def up_y(turn):
        return [(i, i // ys * ys + (i + turn) % ys) for i in range(slice_count)]

    z_turns = (0, 1, 3, 2)

    def along_z(turn):
        return [
            (i, i // chips * chips + ((i // 2 - turn) % zs) * 2 + i % 2) for i in range(panel_count)
        ]

    flip_core = [(i, i ^ 1) for i in range(panel_count)]
    flip_far = [(i, (i + chips) % panel_count) for i in range(panel_count)]
    core = my_panel % 2
    near_z = [
        my_panel // chips * chips + 2 * ((my_panel // 2 + turn) % zs) for turn in z_turns
    ]
    far_z = [(at + chips) % panel_count for at in near_z]
    first = near_z[:1] + far_z[:1] + near_z[1:] + far_z[1:]
    order = jnp.stack(
        [at + core for at in first] + [at + 1 - core for at in first]
    ).astype(i32)

    def pack(blocks, loaded):
        count = len(blocks)
        return pl.pallas_call(
            pack_kernel,
            out_shape=jax.ShapeDtypeStruct((count, rows, width), bf16),
            in_specs=[hbm] * count + [vmem],
            out_specs=hbm,
            scratch_shapes=[sems((count,))],
            compiler_params=params(1),
        )(*blocks, loaded)

    def gather_panels(payload, loaded):
        far = lax.ppermute(payload, "blk", flip_far)
        own = [lax.ppermute(payload, "blk", along_z(turn)) for turn in z_turns[1:]]
        late = [lax.ppermute(far, "blk", along_z(turn)) for turn in z_turns[1:3]]
        late.append(lax.ppermute(own[2], "blk", flip_far))
        own = pack([payload, far] + own + late, loaded)
        return [own], [lax.ppermute(own, "blk", flip_core)]

    flops = 2 * targets * panel_count * per_dev * rank * size * width

    def coder_scratch(n):
        return [pltpu.VMEM((n, rows, width), bf16)]

    far_w, order, ranks, receivers, my_cols, my_count = lax.optimization_barrier(
        (far_w, order, ranks, receivers, my_cols, my_count)
    )

    def load_factors(far_w, far_u):
        return pl.pallas_call(
            load_kernel,
            out_shape=(pltpu.VMEM(far_w.shape, bf16), pltpu.VMEM(far_u.shape, bf16)),
            in_specs=[hbm, hbm],
            out_specs=(vmem, vmem),
            scratch_shapes=[sems((targets,)), sems((targets,))],
            compiler_params=params(34),
            cost_estimate=cost(0, 32),
        )(far_w, far_u)

    def far_products(payload, far_w, far_u):
        held_w, held_u = load_factors(far_w, far_u)
        early, late = gather_panels(payload, held_w)
        n = sum(field.shape[0] for field in early)
        m = panel_count - n
        coded, sums = pl.pallas_call(
            code_kernel,
            out_shape=(
                pltpu.VMEM((targets, n, per_dev * rank, width), bf16),
                jax.ShapeDtypeStruct((EXTRA, width), f32),
            ),
            in_specs=[smem, smem, vmem] + [hbm] * len(early),
            out_specs=(vmem, vmem),
            scratch_shapes=coder_scratch(n) + [sems((n,))],
            compiler_params=params(8),
            cost_estimate=cost(flops * n // panel_count, 16),
        )(order, ranks, held_w, *early)
        around = jax.ShapeDtypeStruct((2 * size + EXTRA, width), bf16)
        return pl.pallas_call(
            far_kernel,
            out_shape=(jax.ShapeDtypeStruct((ys, size, width), bf16),) * 2 + (around,) * ys,
            in_specs=[smem, smem, smem, vmem, vmem, hbm, vmem] + [hbm] * len(late),
            out_specs=(vmem,) * (2 + ys),
            scratch_shapes=coder_scratch(m)
            + [
                pltpu.VMEM((targets, panel_count, per_dev * rank, width), bf16),
                pltpu.VMEM((EXTRA, width), f32),
            ]
            + [sems((m,)), sems((n,))],
            compiler_params=params(18),
            cost_estimate=cost(flops + flops * m // panel_count, 20),
        )(order, ranks, receivers, held_w, held_u, coded, sums, *late)

    def near_products(panel):
        return pl.pallas_call(
            near_kernel,
            out_shape=jax.ShapeDtypeStruct((per_dev, size, width), f32),
            in_specs=[smem, smem, hbm, hbm],
            out_specs=vmem,
            scratch_shapes=[
                pltpu.VMEM((slice_count * per_dev, size, width), bf16),
                pltpu.VMEM((per_dev, slots, size, size), bf16),
                sems((per_dev + 1,)),
            ],
            compiler_params=params(10),
            cost_estimate=cost(2 * per_dev * slots * size * size * width, 5),
        )(my_cols, my_count, tiles, panel)

    def gather_near(blocks):
        return lax.all_gather(blocks, "near", axis=0, tiled=True)

    def scatter_panel(parts, panel):
        cross, stay, *around = parts
        around, own = around[:-1], around[-1]
        cross = lax.ppermute(cross, "near", flip_x)
        around = [lax.ppermute(part, "near", up_y(turn + 1)) for turn, part in enumerate(around)]
        block = (size, width)
        first, *sends, second, send, sums = pl.pallas_call(
            add_kernel,
            out_shape=(jax.ShapeDtypeStruct(block, f32),)
            + (in_hbm(block, bf16),) * (ys - 1)
            + (
                jax.ShapeDtypeStruct(block, f32),
                in_hbm((size + EXTRA, width), bf16),
                jax.ShapeDtypeStruct((2, width), f32),
            ),
            in_specs=[vmem] * (3 + len(around)),
            out_specs=(vmem,) * (ys + 3),
            compiler_params=params(8),
            cost_estimate=cost(0, 3),
        )(stay, cross, own, *around)
        send, panel = lax.optimization_barrier((send, panel))
        sends = [lax.ppermute(part, "near", up_y(turn + 1)) for turn, part in enumerate(sends)]
        return (first, *sends, second, lax.ppermute(send, "near", flip_x), sums), panel

    payload = pl.pallas_call(
        start_kernel,
        grid=(1,),
        out_shape=jax.ShapeDtypeStruct((rows, width), bf16),
        in_specs=[whole(x.shape), whole((per_dev, 1, size, size))],
        out_specs=whole((rows, width)),
        compiler_params=params(60),
    )(x, tiles)
    panel = gather_near(x)
    far_x, panel = scatter_panel(far_products(payload, far_w, far_u), panel)
    image, sums, z, payload = pl.pallas_call(
        functools.partial(middle_kernel, total_rows=total_rows),
        out_shape=(
            in_hbm((per_dev, size, width), f32),
            jax.ShapeDtypeStruct((2, width), f32),
            in_hbm((per_dev, size, width), bf16),
            jax.ShapeDtypeStruct((rows, width), bf16),
        ),
        in_specs=[vmem] * 9,
        out_specs=(vmem,) * 4,
        compiler_params=params(8),
    )(*far_x, near_products(panel), x)
    panel = gather_near(z)
    payload, far_w, far_u = lax.optimization_barrier((payload, far_w, far_u))
    far_z, panel = scatter_panel(far_products(payload, far_w, far_u), panel)
    second_basis, second_image, coefficients = pl.pallas_call(
        functools.partial(last_kernel, total_rows=total_rows),
        out_shape=(
            jax.ShapeDtypeStruct((per_dev, size, width), bf16),
            jax.ShapeDtypeStruct((per_dev, size, width), f32),
            jax.ShapeDtypeStruct((2, width), f32),
        ),
        in_specs=[vmem] * 11,
        out_specs=(vmem, vmem, vmem),
        compiler_params=params(8),
    )(*far_z, near_products(panel), x, image, sums)
    return second_basis[None], second_image[None], coefficients


def solution(mesh):
    placed = (
        P("blk", "near", None, None),
        P("blk", None, "near", None, None),
        P("blk", None, "near", None, None),
        P("blk", None, "near"),
        P("blk", "near", None, None, None),
        P("blk", None, None),
        P("blk", None),
    )
    return jax.shard_map(
        body,
        mesh=mesh,
        in_specs=placed,
        out_specs=(P("blk", "near", None, None), P("blk", "near", None, None), P()),
        check_vma=False,
    )
```

```python
import functools

import jax
import jax.numpy as jnp
from jax import lax
from jax.experimental import pallas as pl
from jax.experimental.pallas import tpu as pltpu
from jax.sharding import PartitionSpec as P

EPS = 1e-06
EXTRA = 16
MIB = 1 << 20


def put_sums(sums, width):
    rows = []
    for value in sums:
        high = value.astype(jnp.bfloat16)
        left = value - high.astype(jnp.float32)
        middle = left.astype(jnp.bfloat16)
        low = (left - middle.astype(jnp.float32)).astype(jnp.bfloat16)
        rows += [high, middle, low]
    rows.append(jnp.zeros((EXTRA - len(rows), width), jnp.bfloat16))
    return jnp.concatenate(rows, axis=0)


def get_sums(rows):
    return (
        rows[0:1] + rows[1:2] + rows[2:3],
        rows[3:4] + rows[4:5] + rows[5:6],
    )


def whole(shape):
    return pl.BlockSpec(shape, lambda *_: (0,) * len(shape))


def start_kernel(x_ref, own_ref, out_ref):
    per_dev, size, width = x_ref.shape
    square = jnp.zeros((1, width), jnp.float32)
    cross = jnp.zeros((1, width), jnp.float32)
    for p in range(per_dev):
        x = x_ref[p]
        x_f = x.astype(jnp.float32)
        image = jnp.dot(own_ref[p, 0], x, preferred_element_type=jnp.float32)
        square += jnp.sum(x_f * x_f, axis=0, keepdims=True)
        cross += jnp.sum(x_f * image, axis=0, keepdims=True)
        out_ref[p * size : (p + 1) * size, :] = x
    out_ref[per_dev * size :, :] = put_sums((square, cross), width)


def load_kernel(w_ref, u_ref, held_w, held_u, w_sem, u_sem):
    copies = []
    for source, target, sems in ((w_ref, held_w, w_sem), (u_ref, held_u, u_sem)):
        copies += [
            pltpu.make_async_copy(source.at[k], target.at[k], sems.at[k])
            for k in range(source.shape[0])
        ]
    for copy in copies:
        copy.start()
    for copy in copies:
        copy.wait()


def pack_kernel(*refs):
    count = len(refs) - 3
    _, out_ref, sems = refs[count:]
    copies = [
        pltpu.make_async_copy(refs[n], out_ref.at[n], sems.at[n]) for n in range(count)
    ]
    for copy in copies:
        copy.start()
    for copy in copies:
        copy.wait()


class Coder:
    def __init__(self, first, order_ref, rank_ref, w_ref, fields, field_buf, field_sem, near=None):
        self.first, self.order_ref, self.rank_ref = first, order_ref, rank_ref
        self.w_ref, self.field_buf, self.near = w_ref, field_buf, near
        parts = [field.at[n] for field in fields for n in range(field.shape[0])]
        self.copies = [
            pltpu.make_async_copy(part, field_buf.at[slot], field_sem.at[slot])
            for slot, part in enumerate(parts)
        ]

    def load(self):
        for copy in self.copies:
            copy.start()

    def run(self, coded_ref, sums_ref, by_panel):
        targets, _, per_dev, rank, size = self.w_ref.shape
        width = coded_ref.shape[3]
        row = lax.broadcasted_iota(jnp.int32, (rank, width), 0)
        for slot, copy in enumerate(self.copies):
            panel = self.order_ref[self.first + slot]
            place = panel if by_panel else slot
            copy.wait()
            sums_ref[...] += self.field_buf[slot, per_dev * size :, :].astype(jnp.float32)
            for p in range(per_dev):
                w = self.w_ref[:, panel, p].reshape(targets * rank, size)
                field = self.field_buf[slot, p * size : (p + 1) * size, :]
                value = jnp.dot(w, field, preferred_element_type=jnp.float32)
                for i in range(targets):
                    live = self.rank_ref[i, p, panel]
                    if slot == 0 and self.near is not None:
                        live = jnp.where(self.near(p, i), 0, live)
                    part = value[i * rank : (i + 1) * rank]
                    part = jnp.where(row < live, part, 0.0).astype(jnp.bfloat16)
                    coded_ref[i, place, p * rank : (p + 1) * rank, :] = part


def code_kernel(order_ref, rank_ref, cols_ref, count_ref, w_ref, *refs):
    fields, (coded_ref, sums_ref, field_buf, field_sem) = refs[:-4], refs[-4:]
    slots = cols_ref.shape[0]
    per_dev = w_ref.shape[2]

    def near(p, i):
        mine = order_ref[order_ref.shape[0] - 1] * per_dev + p
        hit = cols_ref[0, i] == mine
        for k in range(1, slots):
            hit = hit | ((cols_ref[k, i] == mine) & (k < count_ref[i]))
        return hit

    coder = Coder(0, order_ref, rank_ref, w_ref, fields, field_buf, field_sem, near)
    coder.load()
    sums_ref[...] = jnp.zeros_like(sums_ref)
    coder.run(coded_ref, sums_ref, False)


def far_kernel(order_ref, rank_ref, w_ref, u_ref, early_ref, early_sums_ref, *refs):
    fields, refs = refs[:-11], refs[-11:]
    cross_ref, stay_ref, around_refs, near_ref = refs[0], refs[1], refs[2:5], refs[5]
    field_buf, coded_ref, sums_ref, field_sem, early_sem = refs[6:]
    turns = cross_ref.shape[0]
    width = cross_ref.shape[2]
    _, panels, per_dev, _, size = u_ref.shape
    early = early_ref.shape[1]

    def early_copy(slot):
        return pltpu.make_async_copy(
            early_ref.at[:, slot], coded_ref.at[:, order_ref[slot]], early_sem.at[slot]
        )

    coder = Coder(early, order_ref, rank_ref, w_ref, fields, field_buf, field_sem)
    coder.load()
    for slot in range(early):
        early_copy(slot).start()
    sums_ref[...] = early_sums_ref[...]
    coder.run(coded_ref, sums_ref, True)
    extra = put_sums(get_sums(sums_ref[...]), width)
    for slot in range(early):
        early_copy(slot).wait()

    def expand(target):
        u = u_ref[target].reshape(-1, size)
        value = coded_ref[target].reshape(-1, width)
        total = lax.dot_general(
            u, value, (((0,), (0,)), ((), ())), preferred_element_type=jnp.float32
        )
        return total.astype(jnp.bfloat16)

    for turn in range(turns):
        around_ref = near_ref if turn == 0 else around_refs[turn - 1]
        for side, first_ref in ((1, cross_ref), (0, stay_ref)):
            target = order_ref[panels + side * turns + turn] * per_dev
            first_ref[turn] = expand(target)
            around_ref[side * size : (side + 1) * size, :] = expand(target + 1)
        around_ref[2 * size :, :] = extra


def add_kernel(
    stay_ref, cross_ref, near_ref, a1_ref, a2_ref, a3_ref,
    first_ref, s1_ref, s2_ref, s3_ref, second_ref, send_ref, sums_ref,
):
    size = stay_ref.shape[1]
    for turn, out_ref in enumerate((first_ref, s1_ref, s2_ref, s3_ref)):
        total = stay_ref[turn].astype(jnp.float32) + cross_ref[turn].astype(jnp.float32)
        out_ref[...] = total.astype(out_ref.dtype)

    def rows(start, stop):
        total = near_ref[start:stop, :].astype(jnp.float32)
        for ref in (a1_ref, a2_ref, a3_ref):
            total += ref[start:stop, :].astype(jnp.float32)
        return total

    second_ref[...] = rows(0, size)
    send_ref[:size, :] = rows(size, 2 * size).astype(jnp.bfloat16)
    sums = get_sums(rows(2 * size, 2 * size + EXTRA))
    send_ref[size:, :] = put_sums(sums, send_ref.shape[1])
    sums_ref[0:1, :], sums_ref[1:2, :] = sums


def near_kernel(
    order_ref, cols_ref, count_ref, tiles_ref, panel_ref, out_ref, panel_buf, tile_buf, sems
):
    per_dev = out_ref.shape[0]
    copies = [pltpu.make_async_copy(panel_ref, panel_buf, sems.at[per_dev])]
    copies += [
        pltpu.make_async_copy(tiles_ref.at[p], tile_buf.at[p], sems.at[p]) for p in range(per_dev)
    ]
    for copy in copies:
        copy.start()
    for copy in copies:
        copy.wait()
    for p in range(per_dev):
        block = order_ref[order_ref.shape[0] - 1] * per_dev + p
        out_ref[p] = jnp.zeros(out_ref.shape[1:], jnp.float32)
        for k in range(tile_buf.shape[1]):

            @pl.when(k < count_ref[block])
            def _():
                out_ref[p] += jnp.dot(
                    tile_buf[p, k], panel_buf[cols_ref[k, block]], preferred_element_type=jnp.float32
                )


class FarTotal:
    def __init__(self, first_ref, r1_ref, r2_ref, r3_ref, second_ref, cross_ref, sums_ref):
        self.blocks = ((first_ref, r1_ref, r2_ref, r3_ref), (second_ref, cross_ref))
        self.sums_ref = sums_ref

    def block(self, p):
        total, *others = self.blocks[p]
        size = total.shape[0]
        total = total[...]
        for ref in others:
            total += ref[:size, :].astype(jnp.float32)
        return total

    def sums(self):
        cross_ref = self.blocks[1][1]
        size = cross_ref.shape[0] - EXTRA
        came = get_sums(cross_ref[size:, :].astype(jnp.float32))
        return self.sums_ref[0:1, :] + came[0], self.sums_ref[1:2, :] + came[1]


def middle_kernel(*refs, total_rows):
    near_ref, x_ref, image_ref, sums_ref, z_ref, out_ref = refs[7:]
    per_dev, size, width = x_ref.shape
    far = FarTotal(*refs[:7])
    square_x, cross_x = far.sums()
    guess = cross_x / (square_x + EPS * total_rows)
    sums_ref[0:1, :] = square_x
    sums_ref[1:2, :] = guess
    cross = jnp.zeros((1, width), jnp.float32)
    square = jnp.zeros((1, width), jnp.float32)
    for p in range(per_dev):
        image = far.block(p) + near_ref[p]
        image_ref[p] = image
        x = x_ref[p].astype(jnp.float32)
        moved = image - guess * x
        cross += jnp.sum(x * moved, axis=0, keepdims=True)
        square += jnp.sum(moved * moved, axis=0, keepdims=True)
        z = moved.astype(jnp.bfloat16)
        z_ref[p] = z
        out_ref[p * size : (p + 1) * size, :] = z
    out_ref[per_dev * size :, :] = put_sums((cross, square), width)


def last_kernel(*refs, total_rows):
    near_ref, x_ref, image_ref, scale_ref, basis_ref, out_ref, coef_ref = refs[7:]
    per_dev = x_ref.shape[0]
    far = FarTotal(*refs[:7])
    cross, square = far.sums()
    cross, square = cross / total_rows, square / total_rows
    mean_x = scale_ref[0:1, :] / total_rows
    guess = scale_ref[1:2, :]
    scale = lax.rsqrt(mean_x + EPS)
    proj = scale * scale * (cross + guess * mean_x)
    off = proj - guess
    mean_rest = scale * scale * (square - 2.0 * off * cross + off * off * mean_x)
    mean_rest = jnp.maximum(mean_rest, 0.0) + EPS
    factor = scale * lax.rsqrt(mean_rest)
    coef_ref[0:1, :] = proj
    coef_ref[1:2, :] = jnp.sqrt(mean_rest)
    for p in range(per_dev):
        image = image_ref[p]
        x = x_ref[p].astype(jnp.float32)
        basis_ref[p] = ((image - guess * x - off * x) * factor).astype(jnp.bfloat16)
        second = far.block(p) + near_ref[p]
        out_ref[p] = (second - off * image) * factor


def body(rhs_block, far_u, far_w, far_ranks, near_tiles, near_cols, near_count):
    panel_count = lax.axis_size("blk")
    slice_count = lax.axis_size("near")
    my_panel = lax.axis_index("blk")
    my_slice = lax.axis_index("near")
    per_dev, size, width = rhs_block.shape[1:]
    total_rows = float(per_dev * size * panel_count * slice_count)
    slots = near_cols.shape[2]
    targets = far_u.shape[0]
    rank = far_u.shape[3]
    chips = panel_count // 2
    rows = per_dev * size + EXTRA
    bf16, f32, i32 = jnp.bfloat16, jnp.float32, jnp.int32

    x = rhs_block[0]
    tiles = near_tiles[0]
    ranks = far_ranks.transpose(0, 2, 1)
    cols, count = near_cols[0].T, near_count[0]

    hbm = pl.BlockSpec(memory_space=pltpu.HBM)
    smem = pl.BlockSpec(memory_space=pltpu.SMEM)
    vmem = pl.BlockSpec(memory_space=pltpu.VMEM)
    sems = pltpu.SemaphoreType.DMA
    in_hbm = pltpu.HBM

    def params(mib):
        return pltpu.CompilerParams(vmem_limit_bytes=mib * MIB)

    def cost(flops, mib):
        return pl.CostEstimate(flops=flops, bytes_accessed=mib * MIB, transcendentals=0)

    zs = chips // 2
    ys = slice_count // 2
    my_x, my_y = my_slice // ys, my_slice % ys
    receivers = [
        (my_x + side) % 2 * ys + (my_y + turn) % ys for side in range(2) for turn in range(ys)
    ]
    flip_x = [(i, (i + ys) % slice_count) for i in range(slice_count)]

    def up_y(turn):
        return [(i, i // ys * ys + (i + turn) % ys) for i in range(slice_count)]

    z_turns = (0, 1, 3, 2)

    def along_z(turn):
        return [
            (i, i // chips * chips + ((i // 2 - turn) % zs) * 2 + i % 2) for i in range(panel_count)
        ]

    flip_core = [(i, i ^ 1) for i in range(panel_count)]
    flip_far = [(i, (i + chips) % panel_count) for i in range(panel_count)]
    core = my_panel % 2
    near_z = [
        my_panel // chips * chips + 2 * ((my_panel // 2 + turn) % zs) for turn in z_turns
    ]
    far_z = [(at + chips) % panel_count for at in near_z]
    first = near_z[:1] + far_z[:1] + near_z[1:] + far_z[1:]
    order = jnp.stack(
        [at + core for at in first] + [at + 1 - core for at in first] + receivers + [my_slice]
    ).astype(i32)

    def pack(blocks, loaded):
        count = len(blocks)
        return pl.pallas_call(
            pack_kernel,
            out_shape=jax.ShapeDtypeStruct((count, rows, width), bf16),
            in_specs=[hbm] * count + [vmem],
            out_specs=hbm,
            scratch_shapes=[sems((count,))],
            compiler_params=params(1),
        )(*blocks, loaded)

    def gather_panels(payload, loaded):
        far = lax.ppermute(payload, "blk", flip_far)
        own = [lax.ppermute(payload, "blk", along_z(turn)) for turn in z_turns[1:]]
        late = [lax.ppermute(far, "blk", along_z(turn)) for turn in z_turns[1:3]]
        late.append(lax.ppermute(own[2], "blk", flip_far))
        own = pack([payload, far] + own + late, loaded)
        return [own], [lax.ppermute(own, "blk", flip_core)]

    flops = 2 * targets * panel_count * per_dev * rank * size * width

    def coder_scratch(n):
        return [pltpu.VMEM((n, rows, width), bf16)]

    far_w, order, ranks, cols, count = lax.optimization_barrier(
        (far_w, order, ranks, cols, count)
    )

    def load_factors(far_w, far_u):
        return pl.pallas_call(
            load_kernel,
            out_shape=(pltpu.VMEM(far_w.shape, bf16), pltpu.VMEM(far_u.shape, bf16)),
            in_specs=[hbm, hbm],
            out_specs=(vmem, vmem),
            scratch_shapes=[sems((targets,)), sems((targets,))],
            compiler_params=params(34),
            cost_estimate=cost(0, 32),
        )(far_w, far_u)

    def far_products(payload, far_w, far_u):
        held_w, held_u = load_factors(far_w, far_u)
        early, late = gather_panels(payload, held_w)
        n = sum(field.shape[0] for field in early)
        m = panel_count - n
        coded, sums = pl.pallas_call(
            code_kernel,
            out_shape=(
                pltpu.VMEM((targets, n, per_dev * rank, width), bf16),
                jax.ShapeDtypeStruct((EXTRA, width), f32),
            ),
            in_specs=[smem, smem, smem, smem, vmem] + [hbm] * len(early),
            out_specs=(vmem, vmem),
            scratch_shapes=coder_scratch(n) + [sems((n,))],
            compiler_params=params(8),
            cost_estimate=cost(flops * n // panel_count, 16),
        )(order, ranks, cols, count, held_w, *early)
        around = jax.ShapeDtypeStruct((2 * size + EXTRA, width), bf16)
        return pl.pallas_call(
            far_kernel,
            out_shape=(jax.ShapeDtypeStruct((ys, size, width), bf16),) * 2 + (around,) * ys,
            in_specs=[smem, smem, vmem, vmem, hbm, vmem] + [hbm] * len(late),
            out_specs=(vmem,) * (2 + ys),
            scratch_shapes=coder_scratch(m)
            + [
                pltpu.VMEM((targets, panel_count, per_dev * rank, width), bf16),
                pltpu.VMEM((EXTRA, width), f32),
            ]
            + [sems((m,)), sems((n,))],
            compiler_params=params(18),
            cost_estimate=cost(flops + flops * m // panel_count, 20),
        )(order, ranks, held_w, held_u, coded, sums, *late)

    def near_products(panel):
        return pl.pallas_call(
            near_kernel,
            out_shape=jax.ShapeDtypeStruct((per_dev, size, width), f32),
            in_specs=[smem, smem, smem, hbm, hbm],
            out_specs=vmem,
            scratch_shapes=[
                pltpu.VMEM((slice_count * per_dev, size, width), bf16),
                pltpu.VMEM((per_dev, slots, size, size), bf16),
                sems((per_dev + 1,)),
            ],
            compiler_params=params(10),
            cost_estimate=cost(2 * per_dev * slots * size * size * width, 5),
        )(order, cols, count, tiles, panel)

    def gather_near(blocks):
        return lax.all_gather(blocks, "near", axis=0, tiled=True)

    def scatter_panel(parts, panel):
        cross, stay, *around = parts
        around, own = around[:-1], around[-1]
        cross = lax.ppermute(cross, "near", flip_x)
        around = [lax.ppermute(part, "near", up_y(turn + 1)) for turn, part in enumerate(around)]
        block = (size, width)
        first, *sends, second, send, sums = pl.pallas_call(
            add_kernel,
            out_shape=(jax.ShapeDtypeStruct(block, f32),)
            + (in_hbm(block, bf16),) * (ys - 1)
            + (
                jax.ShapeDtypeStruct(block, f32),
                in_hbm((size + EXTRA, width), bf16),
                jax.ShapeDtypeStruct((2, width), f32),
            ),
            in_specs=[vmem] * (3 + len(around)),
            out_specs=(vmem,) * (ys + 3),
            compiler_params=params(8),
            cost_estimate=cost(0, 3),
        )(stay, cross, own, *around)
        send, panel = lax.optimization_barrier((send, panel))
        sends = [lax.ppermute(part, "near", up_y(turn + 1)) for turn, part in enumerate(sends)]
        return (first, *sends, second, lax.ppermute(send, "near", flip_x), sums), panel

    payload = pl.pallas_call(
        start_kernel,
        grid=(1,),
        out_shape=jax.ShapeDtypeStruct((rows, width), bf16),
        in_specs=[whole(x.shape), whole((per_dev, 1, size, size))],
        out_specs=whole((rows, width)),
        compiler_params=params(60),
    )(x, tiles)
    panel = gather_near(x)
    far_x, panel = scatter_panel(far_products(payload, far_w, far_u), panel)
    image, sums, z, payload = pl.pallas_call(
        functools.partial(middle_kernel, total_rows=total_rows),
        out_shape=(
            in_hbm((per_dev, size, width), f32),
            jax.ShapeDtypeStruct((2, width), f32),
            in_hbm((per_dev, size, width), bf16),
            jax.ShapeDtypeStruct((rows, width), bf16),
        ),
        in_specs=[vmem] * 9,
        out_specs=(vmem,) * 4,
        compiler_params=params(8),
    )(*far_x, near_products(panel), x)
    panel = gather_near(z)
    payload, far_w, far_u = lax.optimization_barrier((payload, far_w, far_u))
    far_z, panel = scatter_panel(far_products(payload, far_w, far_u), panel)
    second_basis, second_image, coefficients = pl.pallas_call(
        functools.partial(last_kernel, total_rows=total_rows),
        out_shape=(
            jax.ShapeDtypeStruct((per_dev, size, width), bf16),
            jax.ShapeDtypeStruct((per_dev, size, width), f32),
            jax.ShapeDtypeStruct((2, width), f32),
        ),
        in_specs=[vmem] * 11,
        out_specs=(vmem, vmem, vmem),
        compiler_params=params(8),
    )(*far_z, near_products(panel), x, image, sums)
    return second_basis[None], second_image[None], coefficients


def solution(mesh):
    placed = (
        P("blk", "near", None, None),
        P("blk", None, "near", None, None),
        P("blk", None, "near", None, None),
        P("blk", None, "near"),
        P("blk", "near", None, None, None),
        P("blk", None, None),
        P("blk", None),
    )
    return jax.shard_map(
        body,
        mesh=mesh,
        in_specs=placed,
        out_specs=(P("blk", "near", None, None), P("blk", "near", None, None), P()),
        check_vma=False,
    )
```

```python
import functools

import jax
import jax.numpy as jnp
from jax import lax
from jax.experimental import pallas as pl
from jax.experimental.pallas import tpu as pltpu
from jax.sharding import PartitionSpec as P

EPS = 1e-06
EXTRA = 16
MIB = 1 << 20


def put_sums(sums, width):
    rows = []
    for value in sums:
        high = value.astype(jnp.bfloat16)
        left = value - high.astype(jnp.float32)
        middle = left.astype(jnp.bfloat16)
        low = (left - middle.astype(jnp.float32)).astype(jnp.bfloat16)
        rows += [high, middle, low]
    rows.append(jnp.zeros((EXTRA - len(rows), width), jnp.bfloat16))
    return jnp.concatenate(rows, axis=0)


def get_sums(rows):
    return (
        rows[0:1] + rows[1:2] + rows[2:3],
        rows[3:4] + rows[4:5] + rows[5:6],
    )


def whole(shape):
    return pl.BlockSpec(shape, lambda *_: (0,) * len(shape))


def start_kernel(x_ref, own_ref, out_ref):
    per_dev, size, width = x_ref.shape
    square = jnp.zeros((1, width), jnp.float32)
    cross = jnp.zeros((1, width), jnp.float32)
    for p in range(per_dev):
        x = x_ref[p]
        x_f = x.astype(jnp.float32)
        image = jnp.dot(own_ref[p, 0], x, preferred_element_type=jnp.float32)
        square += jnp.sum(x_f * x_f, axis=0, keepdims=True)
        cross += jnp.sum(x_f * image, axis=0, keepdims=True)
        out_ref[p * size : (p + 1) * size, :] = x
    out_ref[per_dev * size :, :] = put_sums((square, cross), width)


def load_kernel(w_ref, u_ref, held_w, held_u, w_sem, u_sem):
    copies = []
    for source, target, sems in ((w_ref, held_w, w_sem), (u_ref, held_u, u_sem)):
        copies += [
            pltpu.make_async_copy(source.at[k], target.at[k], sems.at[k])
            for k in range(source.shape[0])
        ]
    for copy in copies:
        copy.start()
    for copy in copies:
        copy.wait()


def pack_kernel(*refs):
    count = len(refs) - 3
    _, out_ref, sems = refs[count:]
    copies = [
        pltpu.make_async_copy(refs[n], out_ref.at[n], sems.at[n]) for n in range(count)
    ]
    for copy in copies:
        copy.start()
    for copy in copies:
        copy.wait()


class Coder:
    def __init__(self, first, order_ref, rank_ref, w_ref, fields, field_buf, field_sem, near=None):
        self.first, self.order_ref, self.rank_ref = first, order_ref, rank_ref
        self.w_ref, self.field_buf, self.near = w_ref, field_buf, near
        parts = [field.at[n] for field in fields for n in range(field.shape[0])]
        self.copies = [
            pltpu.make_async_copy(part, field_buf.at[slot], field_sem.at[slot])
            for slot, part in enumerate(parts)
        ]

    def load(self):
        for copy in self.copies:
            copy.start()

    def run(self, coded_ref, sums_ref, by_panel):
        targets, _, per_dev, rank, size = self.w_ref.shape
        width = coded_ref.shape[3]
        row = lax.broadcasted_iota(jnp.int32, (rank, width), 0)
        for slot, copy in enumerate(self.copies):
            panel = self.order_ref[self.first + slot]
            place = panel if by_panel else slot
            copy.wait()
            sums_ref[...] += self.field_buf[slot, per_dev * size :, :].astype(jnp.float32)
            for p in range(per_dev):
                w = self.w_ref[:, panel, p].reshape(targets * rank, size)
                field = self.field_buf[slot, p * size : (p + 1) * size, :]
                value = jnp.dot(w, field, preferred_element_type=jnp.float32)
                for i in range(targets):
                    live = self.rank_ref[i, p, panel]
                    if slot == 0 and self.near is not None:
                        live = jnp.where(self.near(p, i), 0, live)
                    part = value[i * rank : (i + 1) * rank]
                    part = jnp.where(row < live, part, 0.0).astype(jnp.bfloat16)
                    coded_ref[i, place, p * rank : (p + 1) * rank, :] = part


def code_kernel(order_ref, rank_ref, cols_ref, count_ref, w_ref, *refs):
    fields, (coded_ref, sums_ref, field_buf, field_sem) = refs[:-4], refs[-4:]
    slots = cols_ref.shape[0]
    per_dev = w_ref.shape[2]

    def near(p, i):
        mine = order_ref[order_ref.shape[0] - 1] * per_dev + p
        hit = cols_ref[0, i] == mine
        for k in range(1, slots):
            hit = hit | ((cols_ref[k, i] == mine) & (k < count_ref[i]))
        return hit

    coder = Coder(0, order_ref, rank_ref, w_ref, fields, field_buf, field_sem, near)
    coder.load()
    sums_ref[...] = jnp.zeros_like(sums_ref)
    coder.run(coded_ref, sums_ref, False)


def far_kernel(order_ref, rank_ref, w_ref, u_ref, early_ref, early_sums_ref, *refs):
    fields, refs = refs[:-11], refs[-11:]
    cross_ref, stay_ref, around_refs, near_ref = refs[0], refs[1], refs[2:5], refs[5]
    field_buf, coded_ref, sums_ref, field_sem, early_sem = refs[6:]
    turns = cross_ref.shape[0]
    width = cross_ref.shape[2]
    _, panels, per_dev, _, size = u_ref.shape
    early = early_ref.shape[1]

    def early_copy(slot):
        return pltpu.make_async_copy(
            early_ref.at[:, slot], coded_ref.at[:, order_ref[slot]], early_sem.at[slot]
        )

    coder = Coder(early, order_ref, rank_ref, w_ref, fields, field_buf, field_sem)
    coder.load()
    for slot in range(early):
        early_copy(slot).start()
    sums_ref[...] = early_sums_ref[...]
    coder.run(coded_ref, sums_ref, True)
    extra = put_sums(get_sums(sums_ref[...]), width)
    for slot in range(early):
        early_copy(slot).wait()

    def expand(target):
        u = u_ref[target].reshape(-1, size)
        value = coded_ref[target].reshape(-1, width)
        total = lax.dot_general(
            u, value, (((0,), (0,)), ((), ())), preferred_element_type=jnp.float32
        )
        return total.astype(jnp.bfloat16)

    for turn in range(turns):
        around_ref = near_ref if turn == 0 else around_refs[turn - 1]
        for side, first_ref in ((1, cross_ref), (0, stay_ref)):
            target = order_ref[panels + side * turns + turn] * per_dev
            first_ref[turn] = expand(target)
            around_ref[side * size : (side + 1) * size, :] = expand(target + 1)
        around_ref[2 * size :, :] = extra


def add_kernel(
    stay_ref, cross_ref, near_ref, a1_ref, a2_ref, a3_ref,
    first_ref, s1_ref, s2_ref, s3_ref, second_ref, send_ref, sums_ref,
):
    size = stay_ref.shape[1]
    for turn, out_ref in enumerate((first_ref, s1_ref, s2_ref, s3_ref)):
        total = stay_ref[turn].astype(jnp.float32) + cross_ref[turn].astype(jnp.float32)
        out_ref[...] = total.astype(out_ref.dtype)

    def rows(start, stop):
        total = near_ref[start:stop, :].astype(jnp.float32)
        for ref in (a1_ref, a2_ref, a3_ref):
            total += ref[start:stop, :].astype(jnp.float32)
        return total

    second_ref[...] = rows(0, size)
    send_ref[:size, :] = rows(size, 2 * size).astype(jnp.bfloat16)
    sums = get_sums(rows(2 * size, 2 * size + EXTRA))
    send_ref[size:, :] = put_sums(sums, send_ref.shape[1])
    sums_ref[0:1, :], sums_ref[1:2, :] = sums


def near_kernel(
    order_ref, cols_ref, count_ref, tiles_ref, panel_ref, out_ref, panel_buf, tile_buf, sems
):
    per_dev = out_ref.shape[0]
    copies = [pltpu.make_async_copy(panel_ref, panel_buf, sems.at[per_dev])]
    copies += [
        pltpu.make_async_copy(tiles_ref.at[p], tile_buf.at[p], sems.at[p]) for p in range(per_dev)
    ]
    for copy in copies:
        copy.start()
    for copy in copies:
        copy.wait()
    for p in range(per_dev):
        block = order_ref[order_ref.shape[0] - 1] * per_dev + p
        out_ref[p] = jnp.zeros(out_ref.shape[1:], jnp.float32)
        for k in range(tile_buf.shape[1]):

            @pl.when(k < count_ref[block])
            def _():
                out_ref[p] += jnp.dot(
                    tile_buf[p, k], panel_buf[cols_ref[k, block]], preferred_element_type=jnp.float32
                )


class FarTotal:
    def __init__(self, first_ref, r1_ref, r2_ref, r3_ref, second_ref, cross_ref, sums_ref):
        self.blocks = ((first_ref, r1_ref, r2_ref, r3_ref), (second_ref, cross_ref))
        self.sums_ref = sums_ref

    def block(self, p):
        total, *others = self.blocks[p]
        size = total.shape[0]
        total = total[...]
        for ref in others:
            total += ref[:size, :].astype(jnp.float32)
        return total

    def sums(self):
        cross_ref = self.blocks[1][1]
        size = cross_ref.shape[0] - EXTRA
        came = get_sums(cross_ref[size:, :].astype(jnp.float32))
        return self.sums_ref[0:1, :] + came[0], self.sums_ref[1:2, :] + came[1]


def middle_kernel(*refs, total_rows):
    near_ref, x_ref, image_ref, sums_ref, z_ref, out_ref = refs[7:]
    per_dev, size, width = x_ref.shape
    far = FarTotal(*refs[:7])
    square_x, cross_x = far.sums()
    guess = cross_x / (square_x + EPS * total_rows)
    sums_ref[0:1, :] = square_x
    sums_ref[1:2, :] = guess
    cross = jnp.zeros((1, width), jnp.float32)
    square = jnp.zeros((1, width), jnp.float32)
    for p in range(per_dev):
        image = far.block(p) + near_ref[p]
        image_ref[p] = image
        x = x_ref[p].astype(jnp.float32)
        moved = image - guess * x
        cross += jnp.sum(x * moved, axis=0, keepdims=True)
        square += jnp.sum(moved * moved, axis=0, keepdims=True)
        z = moved.astype(jnp.bfloat16)
        z_ref[p] = z
        out_ref[p * size : (p + 1) * size, :] = z
    out_ref[per_dev * size :, :] = put_sums((cross, square), width)


def last_kernel(*refs, total_rows):
    near_ref, x_ref, image_ref, scale_ref, basis_ref, out_ref, coef_ref = refs[7:]
    per_dev = x_ref.shape[0]
    far = FarTotal(*refs[:7])
    cross, square = far.sums()
    cross, square = cross / total_rows, square / total_rows
    mean_x = scale_ref[0:1, :] / total_rows
    guess = scale_ref[1:2, :]
    scale = lax.rsqrt(mean_x + EPS)
    proj = scale * scale * (cross + guess * mean_x)
    off = proj - guess
    mean_rest = scale * scale * (square - 2.0 * off * cross + off * off * mean_x)
    mean_rest = jnp.maximum(mean_rest, 0.0) + EPS
    factor = scale * lax.rsqrt(mean_rest)
    coef_ref[0:1, :] = proj
    coef_ref[1:2, :] = jnp.sqrt(mean_rest)
    for p in range(per_dev):
        image = image_ref[p]
        x = x_ref[p].astype(jnp.float32)
        basis_ref[p] = ((image - guess * x - off * x) * factor).astype(jnp.bfloat16)
        second = far.block(p) + near_ref[p]
        out_ref[p] = (second - off * image) * factor


def body(rhs_block, far_u, far_w, far_ranks, near_tiles, near_cols, near_count):
    panel_count = lax.axis_size("blk")
    slice_count = lax.axis_size("near")
    my_panel = lax.axis_index("blk")
    my_slice = lax.axis_index("near")
    per_dev, size, width = rhs_block.shape[1:]
    total_rows = float(per_dev * size * panel_count * slice_count)
    slots = near_cols.shape[2]
    targets = far_u.shape[0]
    rank = far_u.shape[3]
    chips = panel_count // 2
    rows = per_dev * size + EXTRA
    bf16, f32, i32 = jnp.bfloat16, jnp.float32, jnp.int32

    x = rhs_block[0]
    tiles = near_tiles[0]
    ranks = far_ranks.transpose(0, 2, 1)
    cols, count = near_cols[0].T, near_count[0]

    hbm = pl.BlockSpec(memory_space=pltpu.HBM)
    smem = pl.BlockSpec(memory_space=pltpu.SMEM)
    vmem = pl.BlockSpec(memory_space=pltpu.VMEM)
    sems = pltpu.SemaphoreType.DMA
    in_hbm = pltpu.HBM

    def params(mib):
        return pltpu.CompilerParams(vmem_limit_bytes=mib * MIB)

    def cost(flops, mib):
        return pl.CostEstimate(flops=flops, bytes_accessed=mib * MIB, transcendentals=0)

    zs = chips // 2
    ys = slice_count // 2
    my_x, my_y = my_slice // ys, my_slice % ys
    receivers = [
        (my_x + side) % 2 * ys + (my_y + turn) % ys for side in range(2) for turn in range(ys)
    ]
    flip_x = [(i, (i + ys) % slice_count) for i in range(slice_count)]

    def up_y(turn):
        return [(i, i // ys * ys + (i + turn) % ys) for i in range(slice_count)]

    z_turns = (0, 1, 3, 2)

    def along_z(turn):
        return [
            (i, i // chips * chips + ((i // 2 - turn) % zs) * 2 + i % 2) for i in range(panel_count)
        ]

    flip_core = [(i, i ^ 1) for i in range(panel_count)]
    flip_far = [(i, (i + chips) % panel_count) for i in range(panel_count)]
    core = my_panel % 2
    near_z = [
        my_panel // chips * chips + 2 * ((my_panel // 2 + turn) % zs) for turn in z_turns
    ]
    far_z = [(at + chips) % panel_count for at in near_z]
    first = near_z[:1] + far_z[:1] + near_z[1:] + far_z[1:]
    order = jnp.stack(
        [at + core for at in first] + [at + 1 - core for at in first] + receivers + [my_slice]
    ).astype(i32)

    def pack(blocks, loaded):
        count = len(blocks)
        return pl.pallas_call(
            pack_kernel,
            out_shape=jax.ShapeDtypeStruct((count, rows, width), bf16),
            in_specs=[hbm] * count + [vmem],
            out_specs=hbm,
            scratch_shapes=[sems((count,))],
            compiler_params=params(1),
        )(*blocks, loaded)

    def gather_panels(payload, loaded):
        far = lax.ppermute(payload, "blk", flip_far)
        own = [lax.ppermute(payload, "blk", along_z(turn)) for turn in z_turns[1:]]
        late = [lax.ppermute(far, "blk", along_z(turn)) for turn in z_turns[1:3]]
        late.append(lax.ppermute(own[2], "blk", flip_far))
        own = pack([payload, far] + own + late, loaded)
        return [own], [lax.ppermute(own, "blk", flip_core)]

    flops = 2 * targets * panel_count * per_dev * rank * size * width

    def coder_scratch(n):
        return [pltpu.VMEM((n, rows, width), bf16)]

    far_w, order, ranks, cols, count = lax.optimization_barrier(
        (far_w, order, ranks, cols, count)
    )

    def load_factors(far_w, far_u):
        return pl.pallas_call(
            load_kernel,
            out_shape=(pltpu.VMEM(far_w.shape, bf16), pltpu.VMEM(far_u.shape, bf16)),
            in_specs=[hbm, hbm],
            out_specs=(vmem, vmem),
            scratch_shapes=[sems((targets,)), sems((targets,))],
            compiler_params=params(34),
            cost_estimate=cost(0, 32),
        )(far_w, far_u)

    def far_products(payload, far_w, far_u):
        held_w, held_u = load_factors(far_w, far_u)
        early, late = gather_panels(payload, held_w)
        n = sum(field.shape[0] for field in early)
        m = panel_count - n
        coded, sums = pl.pallas_call(
            code_kernel,
            out_shape=(
                pltpu.VMEM((targets, n, per_dev * rank, width), bf16),
                jax.ShapeDtypeStruct((EXTRA, width), f32),
            ),
            in_specs=[smem, smem, smem, smem, vmem] + [hbm] * len(early),
            out_specs=(vmem, vmem),
            scratch_shapes=coder_scratch(n) + [sems((n,))],
            compiler_params=params(8),
            cost_estimate=cost(flops * n // panel_count, 16),
        )(order, ranks, cols, count, held_w, *early)
        around = jax.ShapeDtypeStruct((2 * size + EXTRA, width), bf16)
        return pl.pallas_call(
            far_kernel,
            out_shape=(jax.ShapeDtypeStruct((ys, size, width), bf16),) * 2 + (around,) * ys,
            in_specs=[smem, smem, vmem, vmem, hbm, vmem] + [hbm] * len(late),
            out_specs=(vmem,) * (2 + ys),
            scratch_shapes=coder_scratch(m)
            + [
                pltpu.VMEM((targets, panel_count, per_dev * rank, width), bf16),
                pltpu.VMEM((EXTRA, width), f32),
            ]
            + [sems((m,)), sems((n,))],
            compiler_params=params(18),
            cost_estimate=cost(flops + flops * m // panel_count, 20),
        )(order, ranks, held_w, held_u, coded, sums, *late)

    def near_products(panel):
        return pl.pallas_call(
            near_kernel,
            out_shape=jax.ShapeDtypeStruct((per_dev, size, width), f32),
            in_specs=[smem, smem, smem, hbm, hbm],
            out_specs=vmem,
            scratch_shapes=[
                pltpu.VMEM((slice_count * per_dev, size, width), bf16),
                pltpu.VMEM((per_dev, slots, size, size), bf16),
                sems((per_dev + 1,)),
            ],
            compiler_params=params(10),
            cost_estimate=cost(2 * per_dev * slots * size * size * width, 5),
        )(order, cols, count, tiles, panel)

    def gather_near(blocks):
        return lax.all_gather(blocks, "near", axis=0, tiled=True)

    def scatter_panel(parts, panel):
        cross, stay, *around = parts
        around, own = around[:-1], around[-1]
        cross = lax.ppermute(cross, "near", flip_x)
        around = [lax.ppermute(part, "near", up_y(turn + 1)) for turn, part in enumerate(around)]
        near = near_products(panel)
        stay, near = lax.optimization_barrier((stay, near))
        block = (size, width)
        first, *sends, second, send, sums = pl.pallas_call(
            add_kernel,
            out_shape=(jax.ShapeDtypeStruct(block, f32),)
            + (in_hbm(block, bf16),) * (ys - 1)
            + (
                jax.ShapeDtypeStruct(block, f32),
                in_hbm((size + EXTRA, width), bf16),
                jax.ShapeDtypeStruct((2, width), f32),
            ),
            in_specs=[vmem] * (3 + len(around)),
            out_specs=(vmem,) * (ys + 3),
            compiler_params=params(8),
            cost_estimate=cost(0, 3),
        )(stay, cross, own, *around)
        sends = [lax.ppermute(part, "near", up_y(turn + 1)) for turn, part in enumerate(sends)]
        return (first, *sends, second, lax.ppermute(send, "near", flip_x), sums), near

    payload = pl.pallas_call(
        start_kernel,
        grid=(1,),
        out_shape=jax.ShapeDtypeStruct((rows, width), bf16),
        in_specs=[whole(x.shape), whole((per_dev, 1, size, size))],
        out_specs=whole((rows, width)),
        compiler_params=params(60),
    )(x, tiles)
    panel = gather_near(x)
    far_x, near_x = scatter_panel(far_products(payload, far_w, far_u), panel)
    image, sums, z, payload = pl.pallas_call(
        functools.partial(middle_kernel, total_rows=total_rows),
        out_shape=(
            in_hbm((per_dev, size, width), f32),
            jax.ShapeDtypeStruct((2, width), f32),
            in_hbm((per_dev, size, width), bf16),
            jax.ShapeDtypeStruct((rows, width), bf16),
        ),
        in_specs=[vmem] * 9,
        out_specs=(vmem,) * 4,
        compiler_params=params(8),
    )(*far_x, near_x, x)
    panel = gather_near(z)
    payload, far_w, far_u = lax.optimization_barrier((payload, far_w, far_u))
    far_z, near_z = scatter_panel(far_products(payload, far_w, far_u), panel)
    second_basis, second_image, coefficients = pl.pallas_call(
        functools.partial(last_kernel, total_rows=total_rows),
        out_shape=(
            jax.ShapeDtypeStruct((per_dev, size, width), bf16),
            jax.ShapeDtypeStruct((per_dev, size, width), f32),
            jax.ShapeDtypeStruct((2, width), f32),
        ),
        in_specs=[vmem] * 11,
        out_specs=(vmem, vmem, vmem),
        compiler_params=params(8),
    )(*far_z, near_z, x, image, sums)
    return second_basis[None], second_image[None], coefficients


def solution(mesh):
    placed = (
        P("blk", "near", None, None),
        P("blk", None, "near", None, None),
        P("blk", None, "near", None, None),
        P("blk", None, "near"),
        P("blk", "near", None, None, None),
        P("blk", None, None),
        P("blk", None),
    )
    return jax.shard_map(
        body,
        mesh=mesh,
        in_specs=placed,
        out_specs=(P("blk", "near", None, None), P("blk", "near", None, None), P()),
        check_vma=False,
    )
```
